32 devices in a mesh: row: 4 (over y, x), col: 8 (over z, core).
Axes of the slice: x: 2, y: 2, z: 4, core: 2. Of those that a mesh axis runs over, the one named last changes fastest.
Arguments:
- excitation: float32 [4, 8, 2, 32, 1024], P('row', 'col'), may hold values from -6 to 6
- shift_real: float32 [4, 8, 1024], P('row', 'col'), may hold values from 6 to 10
- shift_imag: float32 [4, 8, 1024], P('row', 'col'), may hold values from 1.5 to 4
- local_tiles: bfloat16 [4, 8, 8, 4, 128, 128], P('row', 'col'), may hold values from -0.25 to 0.25
- tile_columns: int32 [4, 8, 8, 4], P('row', 'col'), may hold values from 0 to 7
- coupling: bfloat16 [4, 8, 4, 128, 128], P('row', 'col'), may hold values from -0.5 to 0.5
- send_edges: int32 [4, 8, 4, 128], P('row', 'col'), may hold values from 0 to 1023
- receive_edges: int32 [4, 8, 4, 128], P('row', 'col'), may hold values from 0 to 1023
- local_modes: bfloat16 [4, 8, 96, 1024], P('row', 'col'), may hold values from -0.1875 to 0.1875
- coarse_inverse: bfloat16 [3072, 3072], P('row', 'col'), may hold values from -0.15625 to 0.15625
Outputs:
- solution: float32 [4, 8, 2, 32, 1024], P('row', 'col')
- residual: float32 [4, 8, 2, 32, 1024], P('row', 'col')
The draws below stay inside these ranges and needn't reach their ends.
Inputs may be any that keep to these rules, and one draw needn't show every extreme that they name: `tile_columns`: tile column numbers of one subdomain's operator. `send_edges`: edge numbers within the sending subdomain; an edge may repeat. `receive_edges`: edge numbers within the receiving subdomain; an edge may repeat.
All inputs are finite; a program needn't handle non-finite values.
Results may differ from the reference program's by a relative error of at most 0.0003.
Values sent between devices are 32-bit elements; how exact they have to be, the bound alone decides.
A program may use at most 64 MiB of HBM per device.

```python
import jax
import jax.numpy as jnp
from jax import lax

NE = 1024
TILE = 128
BLOCKS = 4
HALO = 128
MODES = 96
SOURCES = 32
OUTER = 2
PASSES = 2
TILE_ROWS = 8
COARSE = 3072
N_ROW = 4
N_COL = 8


def plant(array, own_key, least, high):
    index_at = [jax.random.randint(jax.random.fold_in(own_key, axis), (), 0, length) for axis, length in enumerate(array.shape)]
    widest = array.shape.index(max(array.shape))
    neighbour = index_at[:widest] + [(index_at[widest] + 1) % array.shape[widest]] + index_at[widest + 1:]
    return array.at[tuple(index_at)].set(least).at[tuple(neighbour)].set(high)


def strengthened(values, rng, source, target, parts, factor):
    def block_of(dim):
        return (jnp.arange(values.shape[dim]) // (values.shape[dim] // parts)).reshape((-1,) + (1,) * (values.ndim - 1 - dim))

    near = jax.random.permutation(rng, parts)[block_of(target)]
    far = (block_of(target) + parts // 2) % parts
    return jnp.where((block_of(source) == near) | (block_of(source) == far), factor * values, values)


def block_levels(rng, extent, split, smallest, largest):
    loudness = 1.0
    for dim, parts in split:
        heights = jax.random.uniform(jax.random.fold_in(jax.random.fold_in(rng, 6), dim), (parts,), jnp.float32, smallest / len(split), largest / len(split))
        loudness = loudness * jnp.repeat(jnp.exp(heights), extent[dim] // parts).reshape((-1,) + (1,) * (len(extent) - 1 - dim))
    return loudness


def bell_draw(stream_key, extent, scale, limit, shards=(), kind=jnp.bfloat16):
    drawn = scale * jax.random.normal(stream_key, extent, jnp.float32)
    if shards:
        drawn = drawn * block_levels(stream_key, extent, shards, -0.22, 0.18)
    return jnp.clip(drawn, -limit, limit).astype(kind)


def heavy_noise(key, dims, spread, reach, split, heavy, kind=jnp.bfloat16):
    values = spread * jax.random.normal(key, dims, jnp.float32)
    if split:
        values = values * block_levels(key, dims, split, -0.22, 0.18)
    return jnp.clip(strengthened(values, jax.random.fold_in(key, 3), *heavy), -reach, reach).astype(kind)


def setup_inputs(seed: int = 0) -> dict:
    streams_of = jax.random.split(jax.random.key(seed), 11)
    excitation = bell_draw(streams_of[0], (N_ROW, N_COL, 2, SOURCES, NE), 1.0, 6.0, ((0, 4), (1, 8)), jnp.float32)
    shift_real = jnp.clip(6.0 + 4.0 * jax.random.uniform(streams_of[1], (N_ROW, N_COL, NE), jnp.float32) ** block_levels(streams_of[1], (N_ROW, N_COL, NE), ((0, 4), (1, 8)), -0.2, 0.2), 6.0, 10.0)
    shift_imag = jnp.clip(1.5 + 2.5 * jax.random.uniform(streams_of[2], (N_ROW, N_COL, NE), jnp.float32) ** block_levels(streams_of[2], (N_ROW, N_COL, NE), ((0, 4), (1, 8)), -0.2, 0.2), 1.5, 4.0)
    local_tiles = bell_draw(streams_of[3], (N_ROW, N_COL, TILE_ROWS, BLOCKS, TILE, TILE), (BLOCKS * TILE) ** -0.5, 0.25, ((0, 4), (1, 8)))
    tile_columns = plant(jax.random.randint(streams_of[4], (N_ROW, N_COL, TILE_ROWS, BLOCKS), 0, NE // TILE), jax.random.fold_in(streams_of[4], 1), 0, (NE // TILE) - 1).astype(jnp.int32)
    coupling = bell_draw(streams_of[5], (N_ROW, N_COL, 4, HALO, HALO), HALO ** -0.5, 0.5, ((0, 4), (1, 8)))
    send_edges = plant(jax.random.randint(streams_of[6], (N_ROW, N_COL, 4, HALO), 0, NE), jax.random.fold_in(streams_of[6], 1), 0, NE - 1).astype(jnp.int32)
    receive_edges = plant(jax.random.randint(streams_of[7], (N_ROW, N_COL, 4, HALO), 0, NE), jax.random.fold_in(streams_of[7], 1), 0, NE - 1).astype(jnp.int32)
    local_modes = bell_draw(streams_of[8], (N_ROW, N_COL, MODES, NE), NE ** -0.5, 0.1875, ((0, 4), (1, 8)))
    coarse_inverse = heavy_noise(streams_of[9], (COARSE, COARSE), COARSE ** -0.5, 0.15625, ((0, 4), (1, 8)), (1, 0, 8, 2.0))
    return {"excitation": excitation, "shift_real": shift_real, "shift_imag": shift_imag, "local_tiles": local_tiles, "tile_columns": tile_columns, "coupling": coupling, "send_edges": send_edges, "receive_edges": receive_edges, "local_modes": local_modes, "coarse_inverse": coarse_inverse}


def tile_product(arguments):
    block_tiles, block_columns, vector = arguments
    tile_size = block_tiles.shape[-1]
    row_total = vector.shape[0]
    stacked = vector.reshape(row_total, -1, tile_size)
    picked = stacked[:, block_columns, :]
    result = jnp.einsum("stkb,tkab->sta", picked, block_tiles.astype(picked.dtype), precision=lax.Precision.HIGHEST)
    return result.reshape(row_total, -1)


def shift_grid(packed, axis_number, forward):
    length = packed.shape[axis_number]
    shape_list = list(packed.shape)
    shape_list[axis_number] = 1
    zero_block = jnp.zeros(tuple(shape_list), packed.dtype)
    if forward:
        return jnp.concatenate([zero_block, lax.slice_in_dim(packed, 0, length - 1, axis=axis_number)], axis=axis_number)
    return jnp.concatenate([lax.slice_in_dim(packed, 1, length, axis=axis_number), zero_block], axis=axis_number)


def pick_edges(vector, indices):
    return vector[:, :, indices]


def add_edges(vector, indices, values):
    return vector.at[:, :, indices].add(values)


def operate(field, shift_real, shift_imag, local_tiles, tile_columns, coupling, send_edges, receive_edges):
    grid_rows, grid_cols, halves, count_sources, edge_count = field.shape
    flat_field = field.reshape(grid_rows * grid_cols, halves * count_sources, edge_count)
    flat_tiles = local_tiles.reshape((grid_rows * grid_cols,) + local_tiles.shape[2:])
    flat_columns = tile_columns.reshape((grid_rows * grid_cols,) + tile_columns.shape[2:])
    result = lax.map(tile_product, (flat_tiles, flat_columns, flat_field)).reshape(field.shape)
    outgoing = jax.vmap(jax.vmap(pick_edges))(field, send_edges)
    incoming = [
        shift_grid(outgoing[:, :, :, :, 1, :], 0, True),
        shift_grid(outgoing[:, :, :, :, 0, :], 0, False),
        shift_grid(outgoing[:, :, :, :, 3, :], 1, True),
        shift_grid(outgoing[:, :, :, :, 2, :], 1, False),
    ]
    for direction in range(4):
        contribution = jnp.einsum("ijab,ijpsb->ijpsa", coupling[:, :, direction].astype(field.dtype), incoming[direction], precision=lax.Precision.HIGHEST)
        result = jax.vmap(jax.vmap(add_edges))(result, receive_edges[:, :, direction], contribution)
    real_shift = shift_real[:, :, None, :]
    imag_shift = shift_imag[:, :, None, :]
    real_part = real_shift * field[:, :, 0] - imag_shift * field[:, :, 1]
    imag_part = real_shift * field[:, :, 1] + imag_shift * field[:, :, 0]
    return result + jnp.stack([real_part, imag_part], axis=2)


def relaxed(vector, shift_real, shift_imag):
    real_shift = shift_real[:, :, None, :]
    imag_shift = shift_imag[:, :, None, :]
    modulus = real_shift * real_shift + imag_shift * imag_shift
    real_part = (real_shift * vector[:, :, 0] + imag_shift * vector[:, :, 1]) / modulus
    imag_part = (real_shift * vector[:, :, 1] - imag_shift * vector[:, :, 0]) / modulus
    return jnp.stack([real_part, imag_part], axis=2)


def coarse(residual, local_modes, coarse_inverse):
    grid_rows, grid_cols, halves, count_sources, edge_count = residual.shape
    modes_wide = local_modes.astype(residual.dtype)
    projected = jnp.einsum("ijmn,ijpsn->ijmps", modes_wide, residual, precision=lax.Precision.HIGHEST)
    ordered = jnp.transpose(projected, (1, 0, 2, 3, 4)).reshape(-1, halves * count_sources)
    row_blocks = coarse_inverse.reshape(grid_rows, -1, coarse_inverse.shape[1])

    def block_product(block):
        return jnp.dot(block.astype(ordered.dtype), ordered, precision=lax.Precision.HIGHEST)

    coarse_field = lax.map(block_product, row_blocks).reshape(grid_rows, grid_cols, -1, halves, count_sources)
    return jnp.einsum("ijmn,ijmps->ijpsn", modes_wide, coarse_field, precision=lax.Precision.HIGHEST)


def reference(excitation, shift_real, shift_imag, local_tiles, tile_columns, coupling, send_edges, receive_edges, local_modes, coarse_inverse):
    solution = jnp.zeros_like(excitation)
    residual = excitation
    for repeat in range(OUTER):
        update = coarse(residual, local_modes, coarse_inverse)
        for sweep_index in range(PASSES):
            image = operate(update, shift_real, shift_imag, local_tiles, tile_columns, coupling, send_edges, receive_edges)
            update = update + relaxed(residual - image, shift_real, shift_imag)
        solution = solution + update
        residual = excitation - operate(solution, shift_real, shift_imag, local_tiles, tile_columns, coupling, send_edges, receive_edges)
    return solution, residual
```

```python
import functools

import jax
import jax.numpy as jnp
from jax import lax
from jax.experimental import pallas as pl
from jax.experimental.pallas import tpu as pltpu
from jax.sharding import PartitionSpec as P

OUTER = 2
PASSES = 2
MESH = pl.DeviceIdType.MESH
NT = (((1,), (1,)), ((), ()))
NN = (((1,), (0,)), ((), ()))


def dot(left, right, dims=NN):
    return lax.dot_general(left, right, dims, preferred_element_type=jnp.float32)


def split(value):
    high = value.astype(jnp.bfloat16)
    low = (value - high.astype(jnp.float32)).astype(jnp.bfloat16)
    return jnp.concatenate([high, low], axis=0)


def fold(value):
    half = value.shape[0] // 2
    return value[:half] + value[half:]


def kernel(
    n_row,
    n_col,
    columns,
    send_list,
    receive_list,
    shift_real,
    shift_imag,
    excitation_hbm,
    tiles_hbm,
    coupling_hbm,
    modes_hbm,
    inverse_hbm,
    solution,
    residual,
    tiles,
    coupling,
    modes,
    inverse,
    picker,
    placer,
    field,
    base,
    coarse_in,
    gathered,
    partial,
    reduced,
    halo_out,
    halo_in,
    load_sem,
    gather_send,
    gather_recv,
    reduce_send,
    reduce_recv,
    halo_send,
    halo_recv,
):
    row = lax.axis_index("row")
    col = lax.axis_index("col")
    sources = residual.shape[0]
    half = sources // 2
    blocks, _, tile = field.shape
    per_row = tiles.shape[1]
    mode_count = modes.shape[0]
    pairs = mode_count // 2
    steps_per_outer = PASSES + 1

    loads = [
        pltpu.make_async_copy(source, target, load_sem.at[number])
        for number, (source, target) in enumerate(
            [
                (excitation_hbm, residual),
                (modes_hbm, modes),
                (inverse_hbm, inverse),
                (tiles_hbm, tiles),
                (coupling_hbm, coupling),
            ]
        )
    ]
    for load in loads:
        load.start()

    barrier = pltpu.get_barrier_semaphore()
    for offset in range(1, n_row):
        pl.semaphore_signal(
            barrier, inc=1, device_id={"row": lax.rem(row + offset, n_row)}, device_id_type=MESH
        )
    for offset in range(1, n_col):
        pl.semaphore_signal(
            barrier, inc=1, device_id={"col": lax.rem(col + offset, n_col)}, device_id_type=MESH
        )

    directions = picker.shape[1] // tile
    edge = lax.broadcasted_iota(jnp.int32, (blocks * tile, tile), 0)
    for d in range(directions):
        lanes = slice(d * tile, (d + 1) * tile)
        picker[:, lanes] = (edge == send_list[d : d + 1, :]).astype(jnp.bfloat16)
        placer[:, lanes] = (edge == receive_list[d : d + 1, :]).astype(jnp.bfloat16)
    solution[...] = jnp.zeros_like(solution)

    exists = [row > 0, row < n_row - 1, col > 0, col < n_col - 1]
    target = [{"row": row - 1}, {"row": row + 1}, {"col": col - 1}, {"col": col + 1}]

    for d in range(directions):

        @pl.when(jnp.logical_not(exists[d]))
        def _():
            for k in range(halo_in.shape[0]):
                halo_in[k, d] = jnp.zeros(halo_in.shape[2:], jnp.float32)

    for load in loads:
        load.wait()
    pl.semaphore_wait(barrier, n_row - 1 + n_col - 1)

    lane = lax.broadcasted_iota(jnp.int32, (pairs, 2 * sources), 1)
    first = lane < sources

    def packed(value):
        top, bottom = value[:pairs], value[pairs:]
        other = jnp.where(first, bottom, top)
        return jnp.where(first, top, bottom) + pltpu.roll(other, sources, 1)

    def unpacked(value):
        turned = pltpu.roll(value, sources, 1)
        return jnp.concatenate(
            [jnp.where(first, value, turned), jnp.where(first, turned, value)], axis=0
        )

    def gather_copy(step, offset, slot):
        return pltpu.make_async_remote_copy(
            src_ref=gathered.at[step, slot],
            dst_ref=gathered.at[step, slot],
            send_sem=gather_send.at[step, offset - 1],
            recv_sem=gather_recv.at[step, slot],
            device_id={"row": lax.rem(row + offset, n_row)},
            device_id_type=MESH,
        )

    def reduce_copy(step, offset):
        peer = lax.rem(col + offset, n_col)
        return pltpu.make_async_remote_copy(
            src_ref=partial.at[step, peer],
            dst_ref=reduced.at[step, offset - 1],
            send_sem=reduce_send.at[step, offset - 1],
            recv_sem=reduce_recv.at[step, offset - 1],
            device_id={"col": peer},
            device_id_type=MESH,
        )

    def halo_copy(k, d):
        return pltpu.make_async_remote_copy(
            src_ref=halo_out.at[k, d],
            dst_ref=halo_in.at[k, d ^ 1],
            send_sem=halo_send.at[k, d],
            recv_sem=halo_recv.at[k, d ^ 1],
            device_id=target[d],
            device_id_type=MESH,
        )

    def halo_arrival(k, d):
        return pltpu.make_async_remote_copy(
            src_ref=halo_out.at[k, d],
            dst_ref=halo_in.at[k, d],
            send_sem=halo_send.at[k, d],
            recv_sem=halo_recv.at[k, d],
            device_id=target[d],
            device_id_type=MESH,
        )

    def keep_field(value):
        parts = split(value)
        for b in range(blocks):
            field[b] = parts[:, b * tile : (b + 1) * tile]

    def coarse(step):
        projected = dot(modes[...], split(residual[...]), NT)
        gathered[step, row] = packed(projected)
        for offset in range(1, n_row):
            gather_copy(step, offset, row).start()
        for offset in range(1, n_row):
            gather_copy(step, offset, lax.rem(row + offset, n_row)).wait_recv()
        low_part = lax.broadcasted_iota(jnp.int32, (mode_count, 2 * sources), 1) >= sources
        for i in range(n_row):
            value = unpacked(gathered[step, i])
            high = value.astype(jnp.bfloat16).astype(jnp.float32)
            coarse_in[i * mode_count : (i + 1) * mode_count, :] = jnp.where(
                low_part, value - high, high
            ).astype(jnp.bfloat16)
        for offset in list(range(1, n_col)) + [0]:
            peer = lax.rem(col + offset, n_col)
            partial[step, peer] = packed(dot(inverse[peer], coarse_in[...]))
            if offset:
                reduce_copy(step, offset).start()
        total = partial[step, col]
        for offset in range(1, n_col):
            reduce_copy(step, offset).wait_recv()
            total = total + reduced[step, offset - 1]
        columns_of = unpacked(total)
        padding = jnp.zeros((2 * sources - mode_count, 2 * sources), jnp.float32)
        turned = jnp.concatenate([columns_of, padding], axis=0).T[:sources, :mode_count]
        start = fold(dot(split(turned), modes[...]))
        keep_field(start)
        solution[...] += start
        real, imag = shift_real[...], shift_imag[...]
        base[:half] = residual[:half] - (real * start[:half] - imag * start[half:])
        base[half:] = residual[half:] - (real * start[half:] + imag * start[:half])
        for offset in range(1, n_row):
            gather_copy(step, offset, row).wait_send()
        for offset in range(1, n_col):
            reduce_copy(step, offset).wait_send()

    def body(k, carry):
        step = lax.div(k, steps_per_outer)
        sub = lax.rem(k, steps_per_outer)

        @pl.when(sub == 0)
        def _():
            coarse(step)

        whole = jnp.concatenate([field[b] for b in range(blocks)], axis=1)
        outgoing = fold(dot(whole, picker[...]))
        for d in range(directions):
            halo_out[k, d] = outgoing[:, d * tile : (d + 1) * tile]

            @pl.when(exists[d])
            def _():
                halo_copy(k, d).start()

        for t in range(tiles.shape[0]):
            chosen = jnp.concatenate([field[columns[t, n]] for n in range(per_row)], axis=1)
            stored = jnp.concatenate([tiles[t, n] for n in range(per_row)], axis=1)
            lanes = slice(t * tile, (t + 1) * tile)
            residual[:, lanes] = base[:, lanes] - fold(dot(chosen, stored, NT))

        arrived = []
        for d in range(directions):

            @pl.when(exists[d])
            def _():
                halo_arrival(k, d).wait_recv()

            arrived.append(split(fold(dot(split(halo_in[k, d]), coupling[d], NT))))
        moved = jnp.concatenate(arrived, axis=1)
        result = residual[...] - fold(dot(moved, placer[...], NT))
        residual[...] = result

        @pl.when(sub < PASSES)
        def _():
            real, imag = shift_real[...], shift_imag[...]
            modulus = real * real + imag * imag
            real, imag = real / modulus, imag / modulus
            relaxed = jnp.concatenate(
                [
                    real * result[:half] + imag * result[half:],
                    real * result[half:] - imag * result[:half],
                ],
                axis=0,
            )
            keep_field(relaxed)
            solution[...] += relaxed
            base[...] = jnp.zeros_like(base)

        for d in range(directions):

            @pl.when(exists[d])
            def _():
                halo_copy(k, d).wait_send()

        return carry

    lax.fori_loop(0, OUTER * steps_per_outer, body, 0)


def on_device(
    n_row,
    n_col,
    excitation,
    shift_real,
    shift_imag,
    local_tiles,
    tile_columns,
    coupling,
    send_edges,
    receive_edges,
    local_modes,
    coarse_inverse,
):
    shape = excitation.shape
    edges = shape[-1]
    sources = shape[2] * shape[3]
    tile_rows, per_row, tile, _ = local_tiles.shape[2:]
    directions = send_edges.shape[2]
    mode_count = local_modes.shape[2]
    applies = OUTER * (PASSES + 1)
    vmem = pl.BlockSpec(memory_space=pltpu.VMEM)
    hbm = pl.BlockSpec(memory_space=pl.ANY)
    flat = jax.ShapeDtypeStruct((sources, edges), jnp.float32)
    inverse = coarse_inverse.reshape(n_col, mode_count, coarse_inverse.shape[1])
    results = pl.pallas_call(
        functools.partial(kernel, n_row, n_col),
        out_shape=(flat, flat),
        in_specs=[pl.BlockSpec(memory_space=pltpu.SMEM)] + [vmem] * 4 + [hbm] * 5,
        out_specs=(vmem, vmem),
        scratch_shapes=[
            pltpu.VMEM(local_tiles.shape[2:], jnp.bfloat16),
            pltpu.VMEM(coupling.shape[2:], jnp.bfloat16),
            pltpu.VMEM(local_modes.shape[2:], jnp.bfloat16),
            pltpu.VMEM(inverse.shape, jnp.bfloat16),
            pltpu.VMEM((edges, directions * tile), jnp.bfloat16),
            pltpu.VMEM((edges, directions * tile), jnp.bfloat16),
            pltpu.VMEM((edges // tile, 2 * sources, tile), jnp.bfloat16),
            pltpu.VMEM((sources, edges), jnp.float32),
            pltpu.VMEM((n_row * mode_count, 2 * sources), jnp.bfloat16),
            pltpu.VMEM((OUTER, n_row, mode_count // 2, 2 * sources), jnp.float32),
            pltpu.VMEM((OUTER, n_col, mode_count // 2, 2 * sources), jnp.float32),
            pltpu.VMEM((OUTER, n_col - 1, mode_count // 2, 2 * sources), jnp.float32),
            pltpu.VMEM((applies, directions, sources, tile), jnp.float32),
            pltpu.VMEM((applies, directions, sources, tile), jnp.float32),
            pltpu.SemaphoreType.DMA((5,)),
            pltpu.SemaphoreType.DMA((OUTER, n_row - 1)),
            pltpu.SemaphoreType.DMA((OUTER, n_row)),
            pltpu.SemaphoreType.DMA((OUTER, n_col - 1)),
            pltpu.SemaphoreType.DMA((OUTER, n_col - 1)),
            pltpu.SemaphoreType.DMA((applies, directions)),
            pltpu.SemaphoreType.DMA((applies, directions)),
        ],
        compiler_params=pltpu.CompilerParams(
            collective_id=0, has_side_effects=True, vmem_limit_bytes=40 * 1024 * 1024
        ),
    )(
        tile_columns[0, 0],
        send_edges[0, 0],
        receive_edges[0, 0],
        shift_real[0],
        shift_imag[0],
        excitation.reshape(sources, edges),
        local_tiles[0, 0],
        coupling[0, 0],
        local_modes[0, 0],
        inverse,
    )
    return tuple(value.reshape(shape) for value in results)


def solution(mesh):
    in_specs = (
        P("row", "col", None, None, None),
        P("row", "col", None),
        P("row", "col", None),
        P("row", "col", None, None, None, None),
        P("row", "col", None, None),
        P("row", "col", None, None, None),
        P("row", "col", None, None),
        P("row", "col", None, None),
        P("row", "col", None, None),
        P("row", "col"),
    )
    out_specs = (P("row", "col", None, None, None), P("row", "col", None, None, None))
    return jax.shard_map(
        functools.partial(on_device, mesh.shape["row"], mesh.shape["col"]),
        mesh=mesh,
        in_specs=in_specs,
        out_specs=out_specs,
        check_vma=False,
    )
```

```python
import functools

import jax
import jax.numpy as jnp
from jax import lax
from jax.experimental import pallas as pl
from jax.experimental.pallas import tpu as pltpu
from jax.sharding import PartitionSpec as P

OUTER = 2
PASSES = 2
MESH = pl.DeviceIdType.MESH
NT = (((1,), (1,)), ((), ()))
NN = (((1,), (0,)), ((), ()))


def dot(left, right, dims=NN):
    return lax.dot_general(left, right, dims, preferred_element_type=jnp.float32)


def split(value):
    high = value.astype(jnp.bfloat16)
    low = (value - high.astype(jnp.float32)).astype(jnp.bfloat16)
    return jnp.concatenate([high, low], axis=0)


def fold(value):
    half = value.shape[0] // 2
    return value[:half] + value[half:]


def kernel(
    n_row,
    n_col,
    columns,
    send_list,
    receive_list,
    shift_real,
    shift_imag,
    excitation_hbm,
    tiles_hbm,
    coupling_hbm,
    modes_hbm,
    inverse_hbm,
    solution,
    residual,
    tiles,
    coupling,
    modes,
    inverse,
    picker,
    placer,
    field,
    base,
    coarse_in,
    gathered,
    partial,
    reduced,
    halo_out,
    halo_in,
    load_sem,
    gather_send,
    gather_recv,
    reduce_send,
    reduce_recv,
    halo_send,
    halo_recv,
):
    row = lax.axis_index("row")
    col = lax.axis_index("col")
    sources = residual.shape[0]
    half = sources // 2
    blocks, _, tile = field.shape
    per_row = tiles.shape[1]
    mode_count = modes.shape[0]
    pairs = mode_count // 2
    steps_per_outer = PASSES + 1

    loads = [
        pltpu.make_async_copy(source, target, load_sem.at[number])
        for number, (source, target) in enumerate(
            [
                (excitation_hbm, residual),
                (modes_hbm, modes),
                (inverse_hbm, inverse),
                (tiles_hbm, tiles),
                (coupling_hbm, coupling),
            ]
        )
    ]
    for load in loads:
        load.start()

    barrier = pltpu.get_barrier_semaphore()
    for offset in range(1, n_row):
        pl.semaphore_signal(
            barrier, inc=1, device_id={"row": lax.rem(row + offset, n_row)}, device_id_type=MESH
        )
    for offset in range(1, n_col):
        pl.semaphore_signal(
            barrier, inc=1, device_id={"col": lax.rem(col + offset, n_col)}, device_id_type=MESH
        )

    directions = picker.shape[1] // tile
    solution[...] = jnp.zeros_like(solution)

    exists = [row > 0, row < n_row - 1, col > 0, col < n_col - 1]
    target = [{"row": row - 1}, {"row": row + 1}, {"col": col - 1}, {"col": col + 1}]

    for d in range(directions):

        @pl.when(jnp.logical_not(exists[d]))
        def _():
            for k in range(halo_in.shape[0]):
                halo_in[k, d] = jnp.zeros(halo_in.shape[2:], jnp.float32)

    for load in loads[:2]:
        load.wait()
    pl.semaphore_wait(barrier, n_row - 1 + n_col - 1)

    lane = lax.broadcasted_iota(jnp.int32, (pairs, 2 * sources), 1)
    first = lane < sources

    def packed(value):
        top, bottom = value[:pairs], value[pairs:]
        other = jnp.where(first, bottom, top)
        return jnp.where(first, top, bottom) + pltpu.roll(other, sources, 1)

    def unpacked(value):
        turned = pltpu.roll(value, sources, 1)
        return jnp.concatenate(
            [jnp.where(first, value, turned), jnp.where(first, turned, value)], axis=0
        )

    def gather_copy(step, offset, slot):
        return pltpu.make_async_remote_copy(
            src_ref=gathered.at[step, slot],
            dst_ref=gathered.at[step, slot],
            send_sem=gather_send.at[step, offset - 1],
            recv_sem=gather_recv.at[step, slot],
            device_id={"row": lax.rem(row + offset, n_row)},
            device_id_type=MESH,
        )

    def reduce_copy(step, offset):
        peer = lax.rem(col + offset, n_col)
        return pltpu.make_async_remote_copy(
            src_ref=partial.at[step, peer],
            dst_ref=reduced.at[step, offset - 1],
            send_sem=reduce_send.at[step, offset - 1],
            recv_sem=reduce_recv.at[step, offset - 1],
            device_id={"col": peer},
            device_id_type=MESH,
        )

    def halo_copy(k, d):
        return pltpu.make_async_remote_copy(
            src_ref=halo_out.at[k, d],
            dst_ref=halo_in.at[k, d ^ 1],
            send_sem=halo_send.at[k, d],
            recv_sem=halo_recv.at[k, d ^ 1],
            device_id=target[d],
            device_id_type=MESH,
        )

    def halo_arrival(k, d):
        return pltpu.make_async_remote_copy(
            src_ref=halo_out.at[k, d],
            dst_ref=halo_in.at[k, d],
            send_sem=halo_send.at[k, d],
            recv_sem=halo_recv.at[k, d],
            device_id=target[d],
            device_id_type=MESH,
        )

    def keep_field(value):
        parts = split(value)
        for b in range(blocks):
            field[b] = parts[:, b * tile : (b + 1) * tile]

    def prepare_edges():
        edge = lax.broadcasted_iota(jnp.int32, (blocks * tile, tile), 0)
        along = lax.broadcasted_iota(jnp.int32, (tile, tile), 1)
        for d in range(directions):
            part = slice(d * tile, (d + 1) * tile)
            picker[:, part] = (edge == send_list[d : d + 1, :]).astype(jnp.bfloat16)
            receiver = jnp.broadcast_to(receive_list[d : d + 1, :], (tile, tile)).T
            for b in range(blocks):
                placer[part, b * tile : (b + 1) * tile] = (receiver == along + b * tile).astype(
                    jnp.bfloat16
                )

    def prepare_tiles():
        for load in loads[3:]:
            load.wait()

        def turn(t, carry):
            for n in range(per_row):
                tiles[t, n] = tiles[t, n].T
            return carry

        lax.fori_loop(0, tiles.shape[0], turn, 0)
        for d in range(directions):
            coupling[d] = coupling[d].T

    def coarse(step):
        projected = dot(modes[...], split(residual[...]), NT)
        gathered[step, row] = packed(projected)
        for offset in range(1, n_row):
            gather_copy(step, offset, row).start()

        @pl.when(step == 0)
        def _():
            prepare_edges()
            loads[2].wait()

        for offset in range(1, n_row):
            gather_copy(step, offset, lax.rem(row + offset, n_row)).wait_recv()
        low_part = lax.broadcasted_iota(jnp.int32, (mode_count, 2 * sources), 1) >= sources
        for i in range(n_row):
            value = unpacked(gathered[step, i])
            high = value.astype(jnp.bfloat16).astype(jnp.float32)
            coarse_in[i * mode_count : (i + 1) * mode_count, :] = jnp.where(
                low_part, value - high, high
            ).astype(jnp.bfloat16)
        far_first = sorted(range(1, n_col), key=lambda offset: abs(2 * offset - n_col))
        for offset in far_first + [0]:
            peer = lax.rem(col + offset, n_col)
            partial[step, peer] = packed(dot(inverse[peer], coarse_in[...]))
            if offset:
                reduce_copy(step, offset).start()

        @pl.when(step == 0)
        def _():
            prepare_tiles()

        total = partial[step, col]
        for offset in range(1, n_col):
            reduce_copy(step, offset).wait_recv()
            total = total + reduced[step, offset - 1]
        columns_of = unpacked(total)
        padding = jnp.zeros((2 * sources - mode_count, 2 * sources), jnp.float32)
        turned = jnp.concatenate([columns_of, padding], axis=0).T[:sources, :mode_count]
        start = fold(dot(split(turned), modes[...]))
        keep_field(start)
        solution[...] += start
        real, imag = shift_real[...], shift_imag[...]
        base[:half] = residual[:half] - (real * start[:half] - imag * start[half:])
        base[half:] = residual[half:] - (real * start[half:] + imag * start[:half])
        for offset in range(1, n_row):
            gather_copy(step, offset, row).wait_send()
        for offset in range(1, n_col):
            reduce_copy(step, offset).wait_send()

    def body(k, carry):
        step = lax.div(k, steps_per_outer)
        sub = lax.rem(k, steps_per_outer)

        @pl.when(sub == 0)
        def _():
            coarse(step)

        whole = jnp.concatenate([field[b] for b in range(blocks)], axis=1)
        pairs_of = [range(d, d + 2) for d in range(0, directions, 2)]
        for group in pairs_of:
            span = slice(group[0] * tile, (group[-1] + 1) * tile)
            outgoing = fold(dot(whole, picker[:, span]))
            for place, d in enumerate(group):
                halo_out[k, d] = outgoing[:, place * tile : (place + 1) * tile]

                @pl.when(exists[d])
                def _():
                    halo_copy(k, d).start()

        for t in range(tiles.shape[0]):
            chosen = jnp.concatenate([field[columns[n, t]] for n in range(per_row)], axis=1)
            stored = jnp.concatenate([tiles[t, n] for n in range(per_row)], axis=0)
            lanes = slice(t * tile, (t + 1) * tile)
            residual[:, lanes] = base[:, lanes] - fold(dot(chosen, stored))

        result = residual[...]
        for group in reversed(pairs_of):
            span = slice(group[0] * tile, (group[-1] + 1) * tile)
            for d in group:

                @pl.when(exists[d])
                def _():
                    halo_arrival(k, d).wait_recv()

            arrived = [split(fold(dot(split(halo_in[k, d]), coupling[d]))) for d in group]
            result = result - fold(dot(jnp.concatenate(arrived, axis=1), placer[span, :]))
        residual[...] = result

        @pl.when(sub < PASSES)
        def _():
            real, imag = shift_real[...], shift_imag[...]
            modulus = real * real + imag * imag
            real, imag = real / modulus, imag / modulus
            relaxed = jnp.concatenate(
                [
                    real * result[:half] + imag * result[half:],
                    real * result[half:] - imag * result[:half],
                ],
                axis=0,
            )
            keep_field(relaxed)
            solution[...] += relaxed
            base[...] = jnp.zeros_like(base)

        for d in range(directions):

            @pl.when(exists[d])
            def _():
                halo_copy(k, d).wait_send()

        return carry

    lax.fori_loop(0, OUTER * steps_per_outer, body, 0)


def on_device(
    n_row,
    n_col,
    excitation,
    shift_real,
    shift_imag,
    local_tiles,
    tile_columns,
    coupling,
    send_edges,
    receive_edges,
    local_modes,
    coarse_inverse,
):
    shape = excitation.shape
    edges = shape[-1]
    sources = shape[2] * shape[3]
    tile_rows, per_row, tile, _ = local_tiles.shape[2:]
    directions = send_edges.shape[2]
    mode_count = local_modes.shape[2]
    applies = OUTER * (PASSES + 1)
    vmem = pl.BlockSpec(memory_space=pltpu.VMEM)
    hbm = pl.BlockSpec(memory_space=pl.ANY)
    flat = jax.ShapeDtypeStruct((sources, edges), jnp.float32)
    inverse = coarse_inverse.reshape(n_col, mode_count, coarse_inverse.shape[1])
    results = pl.pallas_call(
        functools.partial(kernel, n_row, n_col),
        out_shape=(flat, flat),
        in_specs=[pl.BlockSpec(memory_space=pltpu.SMEM)] + [vmem] * 4 + [hbm] * 5,
        out_specs=(vmem, vmem),
        scratch_shapes=[
            pltpu.VMEM(local_tiles.shape[2:], jnp.bfloat16),
            pltpu.VMEM(coupling.shape[2:], jnp.bfloat16),
            pltpu.VMEM(local_modes.shape[2:], jnp.bfloat16),
            pltpu.VMEM(inverse.shape, jnp.bfloat16),
            pltpu.VMEM((edges, directions * tile), jnp.bfloat16),
            pltpu.VMEM((directions * tile, edges), jnp.bfloat16),
            pltpu.VMEM((edges // tile, 2 * sources, tile), jnp.bfloat16),
            pltpu.VMEM((sources, edges), jnp.float32),
            pltpu.VMEM((n_row * mode_count, 2 * sources), jnp.bfloat16),
            pltpu.VMEM((OUTER, n_row, mode_count // 2, 2 * sources), jnp.float32),
            pltpu.VMEM((OUTER, n_col, mode_count // 2, 2 * sources), jnp.float32),
            pltpu.VMEM((OUTER, n_col - 1, mode_count // 2, 2 * sources), jnp.float32),
            pltpu.VMEM((applies, directions, sources, tile), jnp.float32),
            pltpu.VMEM((applies, directions, sources, tile), jnp.float32),
            pltpu.SemaphoreType.DMA((5,)),
            pltpu.SemaphoreType.DMA((OUTER, n_row - 1)),
            pltpu.SemaphoreType.DMA((OUTER, n_row)),
            pltpu.SemaphoreType.DMA((OUTER, n_col - 1)),
            pltpu.SemaphoreType.DMA((OUTER, n_col - 1)),
            pltpu.SemaphoreType.DMA((applies, directions)),
            pltpu.SemaphoreType.DMA((applies, directions)),
        ],
        compiler_params=pltpu.CompilerParams(
            collective_id=0, has_side_effects=True, vmem_limit_bytes=63 * 1024 * 1024
        ),
    )(
        tile_columns[0, 0].T,
        send_edges[0, 0],
        receive_edges[0, 0],
        shift_real[0],
        shift_imag[0],
        excitation.reshape(sources, edges),
        local_tiles[0, 0],
        coupling[0, 0],
        local_modes[0, 0],
        inverse,
    )
    return tuple(value.reshape(shape) for value in results)


def solution(mesh):
    in_specs = (
        P("row", "col", None, None, None),
        P("row", "col", None),
        P("row", "col", None),
        P("row", "col", None, None, None, None),
        P("row", "col", None, None),
        P("row", "col", None, None, None),
        P("row", "col", None, None),
        P("row", "col", None, None),
        P("row", "col", None, None),
        P("row", "col"),
    )
    out_specs = (P("row", "col", None, None, None), P("row", "col", None, None, None))
    return jax.shard_map(
        functools.partial(on_device, mesh.shape["row"], mesh.shape["col"]),
        mesh=mesh,
        in_specs=in_specs,
        out_specs=out_specs,
        check_vma=False,
    )
```

```python
import functools

import jax
import jax.numpy as jnp
from jax import lax
from jax.experimental import pallas as pl
from jax.experimental.pallas import tpu as pltpu
from jax.sharding import PartitionSpec as P

OUTER = 2
PASSES = 2
MESH = pl.DeviceIdType.MESH
NT = (((1,), (1,)), ((), ()))
NN = (((1,), (0,)), ((), ()))


def dot(left, right, dims=NN):
    return lax.dot_general(left, right, dims, preferred_element_type=jnp.float32)


def split(value):
    high = value.astype(jnp.bfloat16)
    low = (value - high.astype(jnp.float32)).astype(jnp.bfloat16)
    return jnp.concatenate([high, low], axis=0)


def fold(value):
    half = value.shape[0] // 2
    return value[:half] + value[half:]


def kernel(
    n_row,
    n_col,
    columns,
    send_list,
    receive_list,
    shift_real,
    shift_imag,
    excitation_hbm,
    tiles_hbm,
    coupling_hbm,
    modes_hbm,
    inverse_hbm,
    solution,
    residual,
    tiles,
    coupling,
    modes,
    inverse,
    picker,
    placer,
    field,
    base,
    coarse_in,
    gathered,
    partial,
    shared,
    reduced,
    halo_out,
    halo_in,
    load_sem,
    gather_send,
    gather_recv,
    pair_send,
    pair_recv,
    reduce_send,
    reduce_recv,
    halo_send,
    halo_recv,
):
    row = lax.axis_index("row")
    col = lax.axis_index("col")
    sources = residual.shape[0]
    half = sources // 2
    blocks, _, tile = field.shape
    per_row = tiles.shape[1]
    mode_count = modes.shape[0]
    pairs = mode_count // 2
    steps_per_outer = PASSES + 1

    loads = [
        pltpu.make_async_copy(source, target, load_sem.at[number])
        for number, (source, target) in enumerate(
            [
                (excitation_hbm, residual),
                (modes_hbm, modes),
                (inverse_hbm, inverse),
                (tiles_hbm, tiles),
                (coupling_hbm, coupling),
            ]
        )
    ]
    for load in loads:
        load.start()

    barrier = pltpu.get_barrier_semaphore()
    for offset in range(1, n_row):
        pl.semaphore_signal(
            barrier, inc=1, device_id={"row": lax.rem(row + offset, n_row)}, device_id_type=MESH
        )
    for offset in range(1, n_col):
        pl.semaphore_signal(
            barrier, inc=1, device_id={"col": lax.rem(col + offset, n_col)}, device_id_type=MESH
        )

    directions = picker.shape[1] // tile
    solution[...] = jnp.zeros_like(solution)

    exists = [row > 0, row < n_row - 1, col > 0, col < n_col - 1]
    target = [{"row": row - 1}, {"row": row + 1}, {"col": col - 1}, {"col": col + 1}]

    for d in range(directions):

        @pl.when(jnp.logical_not(exists[d]))
        def _():
            for k in range(halo_in.shape[0]):
                halo_in[k, d] = jnp.zeros(halo_in.shape[2:], jnp.float32)

    lane = lax.broadcasted_iota(jnp.int32, (pairs, 2 * sources), 1)
    first = lane < sources

    def packed(value):
        top, bottom = value[:pairs], value[pairs:]
        other = jnp.where(first, bottom, top)
        return jnp.where(first, top, bottom) + pltpu.roll(other, sources, 1)

    def unpacked(value):
        turned = pltpu.roll(value, sources, 1)
        return jnp.concatenate(
            [jnp.where(first, value, turned), jnp.where(first, turned, value)], axis=0
        )

    def gather_copy(step, offset, slot):
        return pltpu.make_async_remote_copy(
            src_ref=gathered.at[step, slot],
            dst_ref=gathered.at[step, slot],
            send_sem=gather_send.at[step, offset - 1],
            recv_sem=gather_recv.at[step, slot],
            device_id={"row": lax.rem(row + offset, n_row)},
            device_id_type=MESH,
        )

    count = n_col // 2
    pair, member = lax.div(col, 2), lax.rem(col, 2)
    far_first = sorted(range(1, count), key=lambda offset: abs(2 * offset - count)) + [0]

    def pair_copy(step, offset):
        return pltpu.make_async_remote_copy(
            src_ref=partial.at[step, offset, 0],
            dst_ref=shared.at[step, offset],
            send_sem=pair_send.at[step, offset],
            recv_sem=pair_recv.at[step, offset],
            device_id={"col": 2 * pair + 1 - member},
            device_id_type=MESH,
        )

    def reduce_copy(step, offset):
        return pltpu.make_async_remote_copy(
            src_ref=partial.at[step, offset, 1],
            dst_ref=reduced.at[step, offset - 1],
            send_sem=reduce_send.at[step, offset - 1],
            recv_sem=reduce_recv.at[step, offset - 1],
            device_id={"col": 2 * lax.rem(pair + offset, count) + member},
            device_id_type=MESH,
        )

    def halo_copy(k, d):
        return pltpu.make_async_remote_copy(
            src_ref=halo_out.at[k, d],
            dst_ref=halo_in.at[k, d ^ 1],
            send_sem=halo_send.at[k, d],
            recv_sem=halo_recv.at[k, d ^ 1],
            device_id=target[d],
            device_id_type=MESH,
        )

    def halo_arrival(k, d):
        return pltpu.make_async_remote_copy(
            src_ref=halo_out.at[k, d],
            dst_ref=halo_in.at[k, d],
            send_sem=halo_send.at[k, d],
            recv_sem=halo_recv.at[k, d],
            device_id=target[d],
            device_id_type=MESH,
        )

    def keep_field(value):
        parts = split(value)
        for b in range(blocks):
            field[b] = parts[:, b * tile : (b + 1) * tile]

    def project(step):
        gathered[step, row] = packed(dot(modes[...], split(residual[...]), NT))

    for load in loads[:2]:
        load.wait()
    project(0)
    pl.semaphore_wait(barrier, n_row - 1 + n_col - 1)

    def prepare_edges():
        edge = lax.broadcasted_iota(jnp.int32, (blocks * tile, tile), 0)
        along = lax.broadcasted_iota(jnp.int32, (tile, tile), 1)
        for d in range(directions):
            part = slice(d * tile, (d + 1) * tile)
            picker[:, part] = (edge == send_list[d : d + 1, :]).astype(jnp.bfloat16)
            receiver = jnp.broadcast_to(receive_list[d : d + 1, :], (tile, tile)).T
            for b in range(blocks):
                placer[part, b * tile : (b + 1) * tile] = (receiver == along + b * tile).astype(
                    jnp.bfloat16
                )

    def prepare_tiles():
        for load in loads[3:]:
            load.wait()

        def turn(t, carry):
            for n in range(per_row):
                tiles[t, n] = tiles[t, n].T
            return carry

        lax.fori_loop(0, tiles.shape[0], turn, 0)
        for d in range(directions):
            coupling[d] = coupling[d].T

    def coarse(step):
        for offset in range(1, n_row):
            gather_copy(step, offset, row).start()

        @pl.when(step == 0)
        def _():
            prepare_edges()
            loads[2].wait()

        for offset in range(1, n_row):
            gather_copy(step, offset, lax.rem(row + offset, n_row)).wait_recv()
        low_part = lax.broadcasted_iota(jnp.int32, (mode_count, 2 * sources), 1) >= sources
        for i in range(n_row):
            value = unpacked(gathered[step, i])
            high = value.astype(jnp.bfloat16).astype(jnp.float32)
            coarse_in[i * mode_count : (i + 1) * mode_count, :] = jnp.where(
                low_part, value - high, high
            ).astype(jnp.bfloat16)
        for offset in far_first:
            start = 2 * lax.rem(pair + offset, count)
            partial[step, offset, 0] = packed(dot(inverse[start + 1 - member], coarse_in[...]))
            pair_copy(step, offset).start()
        for offset in far_first:
            start = 2 * lax.rem(pair + offset, count)
            own = packed(dot(inverse[start + member], coarse_in[...]))
            pair_copy(step, offset).wait_recv()
            partial[step, offset, 1] = own + shared[step, offset]
            if offset:
                reduce_copy(step, offset).start()

        @pl.when(step == 0)
        def _():
            prepare_tiles()

        total = partial[step, 0, 1]
        for offset in range(1, count):
            reduce_copy(step, offset).wait_recv()
            total = total + reduced[step, offset - 1]
        columns_of = unpacked(total)
        padding = jnp.zeros((2 * sources - mode_count, 2 * sources), jnp.float32)
        turned = jnp.concatenate([columns_of, padding], axis=0).T[:sources, :mode_count]
        start = fold(dot(split(turned), modes[...]))
        keep_field(start)
        solution[...] += start
        real, imag = shift_real[...], shift_imag[...]
        base[:half] = residual[:half] - (real * start[:half] - imag * start[half:])
        base[half:] = residual[half:] - (real * start[half:] + imag * start[:half])
        for offset in range(1, n_row):
            gather_copy(step, offset, row).wait_send()
        for offset in range(1, count):
            reduce_copy(step, offset).wait_send()
        for offset in range(count):
            pair_copy(step, offset).wait_send()

    def body(k, carry):
        step = lax.div(k, steps_per_outer)
        sub = lax.rem(k, steps_per_outer)

        @pl.when(sub == 0)
        def _():
            coarse(step)

        whole = jnp.concatenate([field[b] for b in range(blocks)], axis=1)
        pairs_of = [range(d, d + 2) for d in range(0, directions, 2)]
        for group in pairs_of:
            span = slice(group[0] * tile, (group[-1] + 1) * tile)
            outgoing = fold(dot(whole, picker[:, span]))
            for place, d in enumerate(group):
                halo_out[k, d] = outgoing[:, place * tile : (place + 1) * tile]

                @pl.when(exists[d])
                def _():
                    halo_copy(k, d).start()

        for t in range(tiles.shape[0]):
            chosen = jnp.concatenate([field[columns[n, t]] for n in range(per_row)], axis=1)
            stored = jnp.concatenate([tiles[t, n] for n in range(per_row)], axis=0)
            lanes = slice(t * tile, (t + 1) * tile)
            residual[:, lanes] = base[:, lanes] - fold(dot(chosen, stored))

        result = residual[...]
        for group in reversed(pairs_of):
            span = slice(group[0] * tile, (group[-1] + 1) * tile)
            for d in group:

                @pl.when(exists[d])
                def _():
                    halo_arrival(k, d).wait_recv()

            arrived = [split(fold(dot(split(halo_in[k, d]), coupling[d]))) for d in group]
            result = result - fold(dot(jnp.concatenate(arrived, axis=1), placer[span, :]))
        residual[...] = result

        @pl.when(sub < PASSES)
        def _():
            real, imag = shift_real[...], shift_imag[...]
            modulus = real * real + imag * imag
            real, imag = real / modulus, imag / modulus
            relaxed = jnp.concatenate(
                [
                    real * result[:half] + imag * result[half:],
                    real * result[half:] - imag * result[:half],
                ],
                axis=0,
            )
            keep_field(relaxed)
            solution[...] += relaxed
            base[...] = jnp.zeros_like(base)

        @pl.when(jnp.logical_and(sub == PASSES, step < OUTER - 1))
        def _():
            project(step + 1)

        for d in range(directions):

            @pl.when(exists[d])
            def _():
                halo_copy(k, d).wait_send()

        return carry

    lax.fori_loop(0, OUTER * steps_per_outer, body, 0)


def on_device(
    n_row,
    n_col,
    excitation,
    shift_real,
    shift_imag,
    local_tiles,
    tile_columns,
    coupling,
    send_edges,
    receive_edges,
    local_modes,
    coarse_inverse,
):
    shape = excitation.shape
    edges = shape[-1]
    sources = shape[2] * shape[3]
    tile_rows, per_row, tile, _ = local_tiles.shape[2:]
    directions = send_edges.shape[2]
    mode_count = local_modes.shape[2]
    applies = OUTER * (PASSES + 1)
    vmem = pl.BlockSpec(memory_space=pltpu.VMEM)
    hbm = pl.BlockSpec(memory_space=pl.ANY)
    flat = jax.ShapeDtypeStruct((sources, edges), jnp.float32)
    inverse = coarse_inverse.reshape(n_col, mode_count, coarse_inverse.shape[1])
    results = pl.pallas_call(
        functools.partial(kernel, n_row, n_col),
        out_shape=(flat, flat),
        in_specs=[pl.BlockSpec(memory_space=pltpu.SMEM)] + [vmem] * 4 + [hbm] * 5,
        out_specs=(vmem, vmem),
        scratch_shapes=[
            pltpu.VMEM(local_tiles.shape[2:], jnp.bfloat16),
            pltpu.VMEM(coupling.shape[2:], jnp.bfloat16),
            pltpu.VMEM(local_modes.shape[2:], jnp.bfloat16),
            pltpu.VMEM(inverse.shape, jnp.bfloat16),
            pltpu.VMEM((edges, directions * tile), jnp.bfloat16),
            pltpu.VMEM((directions * tile, edges), jnp.bfloat16),
            pltpu.VMEM((edges // tile, 2 * sources, tile), jnp.bfloat16),
            pltpu.VMEM((sources, edges), jnp.float32),
            pltpu.VMEM((n_row * mode_count, 2 * sources), jnp.bfloat16),
            pltpu.VMEM((OUTER, n_row, mode_count // 2, 2 * sources), jnp.float32),
            pltpu.VMEM((OUTER, n_col // 2, 2, mode_count // 2, 2 * sources), jnp.float32),
            pltpu.VMEM((OUTER, n_col // 2, mode_count // 2, 2 * sources), jnp.float32),
            pltpu.VMEM((OUTER, n_col // 2 - 1, mode_count // 2, 2 * sources), jnp.float32),
            pltpu.VMEM((applies, directions, sources, tile), jnp.float32),
            pltpu.VMEM((applies, directions, sources, tile), jnp.float32),
            pltpu.SemaphoreType.DMA((5,)),
            pltpu.SemaphoreType.DMA((OUTER, n_row - 1)),
            pltpu.SemaphoreType.DMA((OUTER, n_row)),
            pltpu.SemaphoreType.DMA((OUTER, n_col // 2)),
            pltpu.SemaphoreType.DMA((OUTER, n_col // 2)),
            pltpu.SemaphoreType.DMA((OUTER, n_col // 2 - 1)),
            pltpu.SemaphoreType.DMA((OUTER, n_col // 2 - 1)),
            pltpu.SemaphoreType.DMA((applies, directions)),
            pltpu.SemaphoreType.DMA((applies, directions)),
        ],
        compiler_params=pltpu.CompilerParams(
            collective_id=0, has_side_effects=True, vmem_limit_bytes=63 * 1024 * 1024
        ),
    )(
        tile_columns[0, 0].T,
        send_edges[0, 0],
        receive_edges[0, 0],
        shift_real[0],
        shift_imag[0],
        excitation.reshape(sources, edges),
        local_tiles[0, 0],
        coupling[0, 0],
        local_modes[0, 0],
        inverse,
    )
    return tuple(value.reshape(shape) for value in results)


def solution(mesh):
    in_specs = (
        P("row", "col", None, None, None),
        P("row", "col", None),
        P("row", "col", None),
        P("row", "col", None, None, None, None),
        P("row", "col", None, None),
        P("row", "col", None, None, None),
        P("row", "col", None, None),
        P("row", "col", None, None),
        P("row", "col", None, None),
        P("row", "col"),
    )
    out_specs = (P("row", "col", None, None, None), P("row", "col", None, None, None))
    return jax.shard_map(
        functools.partial(on_device, mesh.shape["row"], mesh.shape["col"]),
        mesh=mesh,
        in_specs=in_specs,
        out_specs=out_specs,
        check_vma=False,
    )
```

```python
import functools

import jax
import jax.numpy as jnp
from jax import lax
from jax.experimental import pallas as pl
from jax.experimental.pallas import tpu as pltpu
from jax.sharding import PartitionSpec as P

OUTER = 2
PASSES = 2
MESH = pl.DeviceIdType.MESH
NT = (((1,), (1,)), ((), ()))
NN = (((1,), (0,)), ((), ()))


def dot(left, right, dims=NN):
    return lax.dot_general(left, right, dims, preferred_element_type=jnp.float32)


def split(value):
    high = value.astype(jnp.bfloat16)
    low = (value - high.astype(jnp.float32)).astype(jnp.bfloat16)
    return jnp.concatenate([high, low], axis=0)


def fold(value):
    half = value.shape[0] // 2
    return value[:half] + value[half:]


def kernel(
    n_row,
    n_col,
    columns,
    send_list,
    receive_list,
    shift_real,
    shift_imag,
    excitation_hbm,
    tiles_hbm,
    coupling_hbm,
    modes_hbm,
    inverse_hbm,
    solution,
    residual,
    tiles,
    coupling,
    modes,
    inverse,
    picker,
    placer,
    field,
    base,
    coarse_in,
    gathered,
    partial,
    reduced,
    halo_out,
    halo_in,
    load_sem,
    gather_send,
    gather_recv,
    reduce_send,
    reduce_recv,
    halo_send,
    halo_recv,
):
    row = lax.axis_index("row")
    col = lax.axis_index("col")
    sources = residual.shape[0]
    half = sources // 2
    blocks, _, tile = field.shape
    per_row = tiles.shape[1]
    mode_count = modes.shape[0]
    pairs = mode_count // 2
    steps_per_outer = PASSES + 1

    loads = [
        pltpu.make_async_copy(source, target, load_sem.at[number])
        for number, (source, target) in enumerate(
            [
                (excitation_hbm, residual),
                (modes_hbm, modes),
                (inverse_hbm, inverse),
                (tiles_hbm, tiles),
                (coupling_hbm, coupling),
            ]
        )
    ]
    for load in loads:
        load.start()

    barrier = pltpu.get_barrier_semaphore()
    for offset in range(1, n_row):
        pl.semaphore_signal(
            barrier, inc=1, device_id={"row": lax.rem(row + offset, n_row)}, device_id_type=MESH
        )
    for offset in range(1, n_col):
        pl.semaphore_signal(
            barrier, inc=1, device_id={"col": lax.rem(col + offset, n_col)}, device_id_type=MESH
        )

    directions = picker.shape[1] // tile
    solution[...] = jnp.zeros_like(solution)

    exists = [row > 0, row < n_row - 1, col > 0, col < n_col - 1]
    target = [{"row": row - 1}, {"row": row + 1}, {"col": col - 1}, {"col": col + 1}]

    for d in range(directions):

        @pl.when(jnp.logical_not(exists[d]))
        def _():
            for k in range(halo_in.shape[0]):
                halo_in[k, d] = jnp.zeros(halo_in.shape[2:], jnp.float32)

    lane = lax.broadcasted_iota(jnp.int32, (pairs, 2 * sources), 1)
    first = lane < sources

    def packed(value):
        top, bottom = value[:pairs], value[pairs:]
        other = jnp.where(first, bottom, top)
        return jnp.where(first, top, bottom) + pltpu.roll(other, sources, 1)

    def unpacked(value):
        turned = pltpu.roll(value, sources, 1)
        return jnp.concatenate(
            [jnp.where(first, value, turned), jnp.where(first, turned, value)], axis=0
        )

    def gather_copy(step, offset, slot):
        return pltpu.make_async_remote_copy(
            src_ref=gathered.at[step, slot],
            dst_ref=gathered.at[step, slot],
            send_sem=gather_send.at[step, offset - 1],
            recv_sem=gather_recv.at[step, slot],
            device_id={"row": lax.rem(row + offset, n_row)},
            device_id_type=MESH,
        )

    def reduce_copy(step, offset):
        peer = lax.rem(col + offset, n_col)
        return pltpu.make_async_remote_copy(
            src_ref=partial.at[step, peer],
            dst_ref=reduced.at[step, offset - 1],
            send_sem=reduce_send.at[step, offset - 1],
            recv_sem=reduce_recv.at[step, offset - 1],
            device_id={"col": peer},
            device_id_type=MESH,
        )

    def halo_copy(k, d):
        return pltpu.make_async_remote_copy(
            src_ref=halo_out.at[k, d],
            dst_ref=halo_in.at[k, d ^ 1],
            send_sem=halo_send.at[k, d],
            recv_sem=halo_recv.at[k, d ^ 1],
            device_id=target[d],
            device_id_type=MESH,
        )

    def halo_arrival(k, d):
        return pltpu.make_async_remote_copy(
            src_ref=halo_out.at[k, d],
            dst_ref=halo_in.at[k, d],
            send_sem=halo_send.at[k, d],
            recv_sem=halo_recv.at[k, d],
            device_id=target[d],
            device_id_type=MESH,
        )

    def keep_field(value):
        parts = split(value)
        for b in range(blocks):
            field[b] = parts[:, b * tile : (b + 1) * tile]

    def project(step):
        gathered[step, row] = packed(dot(modes[...], split(residual[...]), NT))

    for load in loads[:2]:
        load.wait()
    project(0)
    pl.semaphore_wait(barrier, n_row - 1 + n_col - 1)

    def prepare_edges():
        along = lax.broadcasted_iota(jnp.int32, (tile, tile), 1)
        down = lax.broadcasted_iota(jnp.int32, (tile, tile), 0)
        receivers = [
            jnp.broadcast_to(receive_list[d : d + 1, :], (tile, tile)).T for d in range(directions)
        ]

        def one_block(b, carry):
            start = pl.multiple_of(b * tile, tile)
            for d in range(directions):
                part = slice(d * tile, (d + 1) * tile)
                picker[pl.ds(start, tile), part] = (
                    down + start == send_list[d : d + 1, :]
                ).astype(jnp.bfloat16)
                placer[part, pl.ds(start, tile)] = (receivers[d] == along + start).astype(
                    jnp.bfloat16
                )
            return carry

        lax.fori_loop(0, blocks, one_block, 0)

    def prepare_tiles():
        for load in loads[3:]:
            load.wait()

        def turn(t, carry):
            for n in range(per_row):
                tiles[t, n] = tiles[t, n].T
            return carry

        lax.fori_loop(0, tiles.shape[0], turn, 0)
        for d in range(directions):
            coupling[d] = coupling[d].T

    def coarse(step):
        for offset in range(1, n_row):
            gather_copy(step, offset, row).start()

        @pl.when(step == 0)
        def _():
            prepare_edges()
            loads[2].wait()

        for offset in range(1, n_row):
            gather_copy(step, offset, lax.rem(row + offset, n_row)).wait_recv()
        low_part = lax.broadcasted_iota(jnp.int32, (mode_count, 2 * sources), 1) >= sources
        for i in range(n_row):
            value = unpacked(gathered[step, i])
            high = value.astype(jnp.bfloat16).astype(jnp.float32)
            coarse_in[i * mode_count : (i + 1) * mode_count, :] = jnp.where(
                low_part, value - high, high
            ).astype(jnp.bfloat16)
        products = dot(inverse[...].reshape(n_col * mode_count, -1), coarse_in[...])
        for j in range(n_col):
            partial[step, j] = packed(products[j * mode_count : (j + 1) * mode_count])
        for offset in sorted(range(1, n_col), key=lambda offset: abs(2 * offset - n_col)):
            reduce_copy(step, offset).start()

        @pl.when(step == 0)
        def _():
            prepare_tiles()

        total = partial[step, col]
        for offset in range(1, n_col):
            reduce_copy(step, offset).wait_recv()
            total = total + reduced[step, offset - 1]
        columns_of = unpacked(total)
        padding = jnp.zeros((2 * sources - mode_count, 2 * sources), jnp.float32)
        turned = jnp.concatenate([columns_of, padding], axis=0).T[:sources, :mode_count]
        start = fold(dot(split(turned), modes[...]))
        keep_field(start)
        solution[...] += start
        real, imag = shift_real[...], shift_imag[...]
        base[:half] = residual[:half] - (real * start[:half] - imag * start[half:])
        base[half:] = residual[half:] - (real * start[half:] + imag * start[:half])
        for offset in range(1, n_row):
            gather_copy(step, offset, row).wait_send()
        for offset in range(1, n_col):
            reduce_copy(step, offset).wait_send()

    def body(k, carry):
        step = lax.div(k, steps_per_outer)
        sub = lax.rem(k, steps_per_outer)

        @pl.when(sub == 0)
        def _():
            coarse(step)

        whole = jnp.concatenate([field[b] for b in range(blocks)], axis=1)
        pairs_of = [range(d, d + 2) for d in range(0, directions, 2)]
        for group in pairs_of:
            span = slice(group[0] * tile, (group[-1] + 1) * tile)
            outgoing = fold(dot(whole, picker[:, span]))
            for place, d in enumerate(group):
                halo_out[k, d] = outgoing[:, place * tile : (place + 1) * tile]

                @pl.when(exists[d])
                def _():
                    halo_copy(k, d).start()

        def local(t, carry):
            chosen = jnp.concatenate([field[columns[n, t]] for n in range(per_row)], axis=1)
            stored = tiles[t].reshape(per_row * tile, tile)
            lanes = pl.ds(pl.multiple_of(t * tile, tile), tile)
            residual[:, lanes] = base[:, lanes] - fold(dot(chosen, stored))
            return carry

        lax.fori_loop(0, tiles.shape[0], local, 0)

        result = residual[...]
        for group in reversed(pairs_of):
            span = slice(group[0] * tile, (group[-1] + 1) * tile)
            for d in group:

                @pl.when(exists[d])
                def _():
                    halo_arrival(k, d).wait_recv()

            arrived = [split(fold(dot(split(halo_in[k, d]), coupling[d]))) for d in group]
            result = result - fold(dot(jnp.concatenate(arrived, axis=1), placer[span, :]))
        residual[...] = result

        @pl.when(sub < PASSES)
        def _():
            real, imag = shift_real[...], shift_imag[...]
            modulus = real * real + imag * imag
            real, imag = real / modulus, imag / modulus
            relaxed = jnp.concatenate(
                [
                    real * result[:half] + imag * result[half:],
                    real * result[half:] - imag * result[:half],
                ],
                axis=0,
            )
            keep_field(relaxed)
            solution[...] += relaxed
            base[...] = jnp.zeros_like(base)

        @pl.when(jnp.logical_and(sub == PASSES, step < OUTER - 1))
        def _():
            project(step + 1)

        for d in range(directions):

            @pl.when(exists[d])
            def _():
                halo_copy(k, d).wait_send()

        return carry

    lax.fori_loop(0, OUTER * steps_per_outer, body, 0)


def on_device(
    n_row,
    n_col,
    excitation,
    shift_real,
    shift_imag,
    local_tiles,
    tile_columns,
    coupling,
    send_edges,
    receive_edges,
    local_modes,
    coarse_inverse,
):
    shape = excitation.shape
    edges = shape[-1]
    sources = shape[2] * shape[3]
    tile_rows, per_row, tile, _ = local_tiles.shape[2:]
    directions = send_edges.shape[2]
    mode_count = local_modes.shape[2]
    applies = OUTER * (PASSES + 1)
    vmem = pl.BlockSpec(memory_space=pltpu.VMEM)
    hbm = pl.BlockSpec(memory_space=pl.ANY)
    flat = jax.ShapeDtypeStruct((sources, edges), jnp.float32)
    inverse = coarse_inverse.reshape(n_col, mode_count, coarse_inverse.shape[1])
    results = pl.pallas_call(
        functools.partial(kernel, n_row, n_col),
        out_shape=(flat, flat),
        in_specs=[pl.BlockSpec(memory_space=pltpu.SMEM)] + [vmem] * 4 + [hbm] * 5,
        out_specs=(vmem, vmem),
        scratch_shapes=[
            pltpu.VMEM(local_tiles.shape[2:], jnp.bfloat16),
            pltpu.VMEM(coupling.shape[2:], jnp.bfloat16),
            pltpu.VMEM(local_modes.shape[2:], jnp.bfloat16),
            pltpu.VMEM(inverse.shape, jnp.bfloat16),
            pltpu.VMEM((edges, directions * tile), jnp.bfloat16),
            pltpu.VMEM((directions * tile, edges), jnp.bfloat16),
            pltpu.VMEM((edges // tile, 2 * sources, tile), jnp.bfloat16),
            pltpu.VMEM((sources, edges), jnp.float32),
            pltpu.VMEM((n_row * mode_count, 2 * sources), jnp.bfloat16),
            pltpu.VMEM((OUTER, n_row, mode_count // 2, 2 * sources), jnp.float32),
            pltpu.VMEM((OUTER, n_col, mode_count // 2, 2 * sources), jnp.float32),
            pltpu.VMEM((OUTER, n_col - 1, mode_count // 2, 2 * sources), jnp.float32),
            pltpu.VMEM((applies, directions, sources, tile), jnp.float32),
            pltpu.VMEM((applies, directions, sources, tile), jnp.float32),
            pltpu.SemaphoreType.DMA((5,)),
            pltpu.SemaphoreType.DMA((OUTER, n_row - 1)),
            pltpu.SemaphoreType.DMA((OUTER, n_row)),
            pltpu.SemaphoreType.DMA((OUTER, n_col - 1)),
            pltpu.SemaphoreType.DMA((OUTER, n_col - 1)),
            pltpu.SemaphoreType.DMA((applies, directions)),
            pltpu.SemaphoreType.DMA((applies, directions)),
        ],
        compiler_params=pltpu.CompilerParams(
            collective_id=0, has_side_effects=True, vmem_limit_bytes=63 * 1024 * 1024
        ),
    )(
        tile_columns[0, 0].T,
        send_edges[0, 0],
        receive_edges[0, 0],
        shift_real[0],
        shift_imag[0],
        excitation.reshape(sources, edges),
        local_tiles[0, 0],
        coupling[0, 0],
        local_modes[0, 0],
        inverse,
    )
    return tuple(value.reshape(shape) for value in results)


def solution(mesh):
    in_specs = (
        P("row", "col", None, None, None),
        P("row", "col", None),
        P("row", "col", None),
        P("row", "col", None, None, None, None),
        P("row", "col", None, None),
        P("row", "col", None, None, None),
        P("row", "col", None, None),
        P("row", "col", None, None),
        P("row", "col", None, None),
        P("row", "col"),
    )
    out_specs = (P("row", "col", None, None, None), P("row", "col", None, None, None))
    return jax.shard_map(
        functools.partial(on_device, mesh.shape["row"], mesh.shape["col"]),
        mesh=mesh,
        in_specs=in_specs,
        out_specs=out_specs,
        check_vma=False,
    )
```

```python
import functools

import jax
import jax.numpy as jnp
from jax import lax
from jax.experimental import pallas as pl
from jax.experimental.pallas import tpu as pltpu
from jax.sharding import PartitionSpec as P

OUTER = 2
PASSES = 2
GROUPS = 2
MESH = pl.DeviceIdType.MESH
NT = (((1,), (1,)), ((), ()))
NN = (((1,), (0,)), ((), ()))


def dot(left, right, dims=NN):
    return lax.dot_general(left, right, dims, preferred_element_type=jnp.float32)


def split(value):
    high = value.astype(jnp.bfloat16)
    low = (value - high.astype(jnp.float32)).astype(jnp.bfloat16)
    return jnp.concatenate([high, low], axis=0)


def fold(value):
    half = value.shape[0] // 2
    return value[:half] + value[half:]


def kernel(
    n_row,
    n_col,
    columns,
    send_list,
    receive_list,
    shift_real,
    shift_imag,
    excitation_hbm,
    tiles_hbm,
    coupling_hbm,
    modes_hbm,
    inverse_hbm,
    solution_hbm,
    residual_hbm,
    solution,
    residual,
    tiles,
    coupling,
    modes,
    modes_turned,
    inverse,
    inverse_turned,
    picker,
    placer,
    field,
    base,
    gathered,
    partial,
    reduced,
    halo_out,
    halo_in,
    load_sem,
    store_sem,
    gather_send,
    gather_recv,
    reduce_send,
    reduce_recv,
    halo_send,
    halo_recv,
):
    row = lax.axis_index("row")
    col = lax.axis_index("col")
    groups, sources, _ = residual.shape
    half = sources // 2
    _, blocks, _, tile = field.shape
    per_row = tiles.shape[1]
    directions = halo_in.shape[2]
    applies = halo_in.shape[0]
    mode_count = modes_hbm.shape[0]
    padded = modes.shape[0]
    steps_per_outer = PASSES + 1

    def state_copies(source, target, sems, reverse):
        copies = []
        for g in range(groups):
            for p in range(2):
                whole = source.at[p, pl.ds(g * half, half), :]
                part = target.at[g, pl.ds(p * half, half), :]
                first, second = (part, whole) if reverse else (whole, part)
                copies.append(pltpu.make_async_copy(first, second, sems.at[2 * g + p]))
        return copies

    early = state_copies(excitation_hbm, residual, load_sem, False)
    number = len(early)
    early.append(
        pltpu.make_async_copy(modes_hbm, modes.at[pl.ds(0, mode_count), :], load_sem.at[number])
    )
    late = [
        pltpu.make_async_copy(source, target, load_sem.at[number + 1 + place])
        for place, (source, target) in enumerate(
            [(inverse_hbm, inverse), (tiles_hbm, tiles), (coupling_hbm, coupling)]
        )
    ]
    for load in early + late:
        load.start()

    barrier = pltpu.get_barrier_semaphore()
    for offset in range(1, n_row):
        pl.semaphore_signal(
            barrier, inc=1, device_id={"row": lax.rem(row + offset, n_row)}, device_id_type=MESH
        )
    for offset in range(1, n_col):
        pl.semaphore_signal(
            barrier, inc=1, device_id={"col": lax.rem(col + offset, n_col)}, device_id_type=MESH
        )

    exists = [row > 0, row < n_row - 1, col > 0, col < n_col - 1]
    target = [{"row": row - 1}, {"row": row + 1}, {"col": col - 1}, {"col": col + 1}]

    solution[...] = jnp.zeros_like(solution)
    modes[mode_count:, :] = jnp.zeros((padded - mode_count, modes.shape[1]), jnp.bfloat16)
    for d in range(directions):

        @pl.when(jnp.logical_not(exists[d]))
        def _():
            for k in range(applies):
                for g in range(groups):
                    halo_in[k, g, d] = jnp.zeros(halo_in.shape[3:], jnp.float32)

    def gather_copy(step, g, offset, slot):
        return pltpu.make_async_remote_copy(
            src_ref=gathered.at[step, g, slot],
            dst_ref=gathered.at[step, g, slot],
            send_sem=gather_send.at[step, g, offset - 1],
            recv_sem=gather_recv.at[step, g, slot],
            device_id={"row": lax.rem(row + offset, n_row)},
            device_id_type=MESH,
        )

    def reduce_copy(step, g, offset):
        peer = lax.rem(col + offset, n_col)
        return pltpu.make_async_remote_copy(
            src_ref=partial.at[step, g, peer],
            dst_ref=reduced.at[step, g, offset - 1],
            send_sem=reduce_send.at[step, g, offset - 1],
            recv_sem=reduce_recv.at[step, g, offset - 1],
            device_id={"col": peer},
            device_id_type=MESH,
        )

    def halo_copy(k, g, d, slot):
        return pltpu.make_async_remote_copy(
            src_ref=halo_out.at[k, g, d],
            dst_ref=halo_in.at[k, g, slot],
            send_sem=halo_send.at[k, g, d],
            recv_sem=halo_recv.at[k, g, slot],
            device_id=target[d],
            device_id_type=MESH,
        )

    def gather_start(step, g):
        for offset in range(1, n_row):
            gather_copy(step, g, offset, row).start()

    for load in early:
        load.wait()
    for g in range(groups):
        gathered[0, g, row] = fold(dot(split(residual[g]), modes[...], NT))
    pl.semaphore_wait(barrier, n_row - 1 + n_col - 1)
    for g in range(groups):
        gather_start(0, g)

    def prepare_first():
        late[0].wait()
        blank = jnp.zeros((padded - mode_count, inverse.shape[2]), jnp.bfloat16)

        def turn(j, carry):
            block = jnp.concatenate([inverse[j], blank], axis=0).T
            inverse_turned[:, pl.ds(pl.multiple_of(j * padded, padded), padded)] = block
            return carry

        lax.fori_loop(0, n_col, turn, 0)

    def prepare_edges():
        along = lax.broadcasted_iota(jnp.int32, (tile, tile), 1)
        down = lax.broadcasted_iota(jnp.int32, (tile, tile), 0)
        receivers = [
            jnp.broadcast_to(receive_list[d : d + 1, :], (tile, tile)).T for d in range(directions)
        ]

        def one_block(b, carry):
            start = pl.multiple_of(b * tile, tile)
            for d in range(directions):
                part = slice(d * tile, (d + 1) * tile)
                picker[pl.ds(start, tile), part] = (
                    down + start == send_list[d : d + 1, :]
                ).astype(jnp.bfloat16)
                placer[part, pl.ds(start, tile)] = (receivers[d] == along + start).astype(
                    jnp.bfloat16
                )
            return carry

        lax.fori_loop(0, blocks, one_block, 0)

    def prepare_rest():
        for load in late[1:]:
            load.wait()

        def turn(t, carry):
            for n in range(per_row):
                tiles[t, n] = tiles[t, n].T
            return carry

        lax.fori_loop(0, tiles.shape[0], turn, 0)
        for d in range(directions):
            coupling[d] = coupling[d].T
        for b in range(blocks):
            part = slice(b * tile, (b + 1) * tile)
            modes_turned[part, :] = modes[:, part].T

    def send_field(k, g, value):
        parts = split(value)
        for b in range(blocks):
            field[g, b] = parts[:, b * tile : (b + 1) * tile]
        for first in range(0, directions, 2):
            outgoing = fold(dot(parts, picker[:, first * tile : (first + 2) * tile]))
            for d in (first, first + 1):
                halo_out[k, g, d] = outgoing[:, (d - first) * tile : (d - first + 1) * tile]

                @pl.when(exists[d])
                def _():
                    halo_copy(k, g, d, d ^ 1).start()

    def coarse_product(step, g):
        for offset in range(1, n_row):
            gather_copy(step, g, offset, lax.rem(row + offset, n_row)).wait_recv()
        whole = jnp.concatenate(
            [gathered[step, g, i][:, :mode_count] for i in range(n_row)], axis=1
        )
        products = fold(dot(split(whole), inverse_turned[...]))
        for j in range(n_col):
            partial[step, g, j] = products[:, j * padded : (j + 1) * padded]
        for offset in sorted(range(1, n_col), key=lambda offset: abs(2 * offset - n_col)):
            reduce_copy(step, g, offset).start()

    def coarse_start(step, k, g):
        total = partial[step, g, col]
        for offset in range(1, n_col):
            reduce_copy(step, g, offset).wait_recv()
            total = total + reduced[step, g, offset - 1]
        start = fold(dot(split(total), modes[...]))
        send_field(k, g, start)
        solution[g] += start
        real, imag = shift_real[...], shift_imag[...]
        old = residual[g]
        base[g, :half] = old[:half] - (real * start[:half] - imag * start[half:])
        base[g, half:] = old[half:] - (real * start[half:] + imag * start[:half])

    def apply(step, sub, k, g):
        def local(t, carry):
            chosen = jnp.concatenate([field[g, columns[n, t]] for n in range(per_row)], axis=1)
            stored = tiles[t].reshape(per_row * tile, tile)
            lanes = pl.ds(pl.multiple_of(t * tile, tile), tile)
            residual[g, :, lanes] = base[g, :, lanes] - fold(dot(chosen, stored))
            return carry

        lax.fori_loop(0, tiles.shape[0], local, 0, unroll=2)

        result = residual[g]
        for first in range(directions - 2, -1, -2):
            arrived = []
            for d in (first, first + 1):

                @pl.when(exists[d])
                def _():
                    halo_copy(k, g, d, d).wait_recv()

            for d in (first, first + 1):
                arrived.append(split(fold(dot(split(halo_in[k, g, d]), coupling[d]))))
            span = slice(first * tile, (first + 2) * tile)
            result = result - fold(dot(jnp.concatenate(arrived, axis=1), placer[span, :]))
        residual[g] = result

        @pl.when(sub < PASSES)
        def _():
            real, imag = shift_real[...], shift_imag[...]
            modulus = real * real + imag * imag
            real, imag = real / modulus, imag / modulus
            relaxed = jnp.concatenate(
                [
                    real * result[:half] + imag * result[half:],
                    real * result[half:] - imag * result[:half],
                ],
                axis=0,
            )
            send_field(k + 1, g, relaxed)
            solution[g] += relaxed
            base[g] = jnp.zeros(base.shape[1:], jnp.float32)

        @pl.when(jnp.logical_and(sub == PASSES, step < OUTER - 1))
        def _():
            gathered[step + 1, g, row] = fold(dot(split(result), modes_turned[...]))
            gather_start(step + 1, g)

    def each_group(action):
        def run(g, carry):
            action(g)
            return carry

        lax.fori_loop(0, groups, run, 0)

    def body(k, carry):
        step = lax.div(k, steps_per_outer)
        sub = lax.rem(k, steps_per_outer)

        @pl.when(k == 0)
        def _():
            prepare_first()
            prepare_edges()

        @pl.when(sub == 0)
        def _():
            each_group(lambda g: coarse_product(step, g))

        @pl.when(k == 0)
        def _():
            prepare_rest()

        @pl.when(sub == 0)
        def _():
            each_group(lambda g: coarse_start(step, k, g))

        each_group(lambda g: apply(step, sub, k, g))
        return carry

    lax.fori_loop(0, applies, body, 0)

    stores = state_copies(residual_hbm, residual, store_sem.at[0], True)
    stores += state_copies(solution_hbm, solution, store_sem.at[1], True)
    for store in stores:
        store.start()

    def finish(g):
        for step in range(OUTER):
            for offset in range(1, n_row):
                gather_copy(step, g, offset, row).wait_send()
            for offset in range(1, n_col):
                reduce_copy(step, g, offset).wait_send()
        for d in range(directions):

            @pl.when(exists[d])
            def _():
                for k in range(applies):
                    halo_copy(k, g, d, d ^ 1).wait_send()

    each_group(finish)
    for store in stores:
        store.wait()


def on_device(
    n_row,
    n_col,
    excitation,
    shift_real,
    shift_imag,
    local_tiles,
    tile_columns,
    coupling,
    send_edges,
    receive_edges,
    local_modes,
    coarse_inverse,
):
    shape = excitation.shape
    edges = shape[-1]
    sources = shape[2] * shape[3] // GROUPS
    tile_rows, per_row, tile, _ = local_tiles.shape[2:]
    directions = send_edges.shape[2]
    mode_count = local_modes.shape[2]
    padded = -(-mode_count // tile) * tile
    applies = OUTER * (PASSES + 1)
    vmem = pl.BlockSpec(memory_space=pltpu.VMEM)
    hbm = pl.BlockSpec(memory_space=pl.ANY)
    flat = jax.ShapeDtypeStruct(shape[2:], jnp.float32)
    state = pltpu.VMEM((GROUPS, sources, edges), jnp.float32)
    halo = pltpu.VMEM((applies, GROUPS, directions, sources, tile), jnp.float32)
    inverse = coarse_inverse.reshape(n_col, mode_count, coarse_inverse.shape[1])
    results = pl.pallas_call(
        functools.partial(kernel, n_row, n_col),
        out_shape=(flat, flat),
        in_specs=[pl.BlockSpec(memory_space=pltpu.SMEM)] + [vmem] * 4 + [hbm] * 5,
        out_specs=(hbm, hbm),
        scratch_shapes=[
            state,
            state,
            pltpu.VMEM(local_tiles.shape[2:], jnp.bfloat16),
            pltpu.VMEM(coupling.shape[2:], jnp.bfloat16),
            pltpu.VMEM((padded, edges), jnp.bfloat16),
            pltpu.VMEM((edges, padded), jnp.bfloat16),
            pltpu.VMEM(inverse.shape, jnp.bfloat16),
            pltpu.VMEM((inverse.shape[2], n_col * padded), jnp.bfloat16),
            pltpu.VMEM((edges, directions * tile), jnp.bfloat16),
            pltpu.VMEM((directions * tile, edges), jnp.bfloat16),
            pltpu.VMEM((GROUPS, edges // tile, 2 * sources, tile), jnp.bfloat16),
            state,
            pltpu.VMEM((OUTER, GROUPS, n_row, sources, padded), jnp.float32),
            pltpu.VMEM((OUTER, GROUPS, n_col, sources, padded), jnp.float32),
            pltpu.VMEM((OUTER, GROUPS, n_col - 1, sources, padded), jnp.float32),
            halo,
            halo,
            pltpu.SemaphoreType.DMA((2 * GROUPS + 4,)),
            pltpu.SemaphoreType.DMA((2, 2 * GROUPS)),
            pltpu.SemaphoreType.DMA((OUTER, GROUPS, n_row - 1)),
            pltpu.SemaphoreType.DMA((OUTER, GROUPS, n_row)),
            pltpu.SemaphoreType.DMA((OUTER, GROUPS, n_col - 1)),
            pltpu.SemaphoreType.DMA((OUTER, GROUPS, n_col - 1)),
            pltpu.SemaphoreType.DMA((applies, GROUPS, directions)),
            pltpu.SemaphoreType.DMA((applies, GROUPS, directions)),
        ],
        compiler_params=pltpu.CompilerParams(
            collective_id=0, has_side_effects=True, vmem_limit_bytes=63 * 1024 * 1024
        ),
    )(
        tile_columns[0, 0].T,
        send_edges[0, 0],
        receive_edges[0, 0],
        shift_real[0],
        shift_imag[0],
        excitation[0, 0],
        local_tiles[0, 0],
        coupling[0, 0],
        local_modes[0, 0],
        inverse,
    )
    return tuple(value.reshape(shape) for value in results)


def solution(mesh):
    in_specs = (
        P("row", "col", None, None, None),
        P("row", "col", None),
        P("row", "col", None),
        P("row", "col", None, None, None, None),
        P("row", "col", None, None),
        P("row", "col", None, None, None),
        P("row", "col", None, None),
        P("row", "col", None, None),
        P("row", "col", None, None),
        P("row", "col"),
    )
    out_specs = (P("row", "col", None, None, None), P("row", "col", None, None, None))
    return jax.shard_map(
        functools.partial(on_device, mesh.shape["row"], mesh.shape["col"]),
        mesh=mesh,
        in_specs=in_specs,
        out_specs=out_specs,
        check_vma=False,
    )
```

```python
import functools

import jax
import jax.numpy as jnp
from jax import lax
from jax.experimental import pallas as pl
from jax.experimental.pallas import tpu as pltpu
from jax.sharding import PartitionSpec as P

OUTER = 2
PASSES = 2
GROUPS = 2
MESH = pl.DeviceIdType.MESH
NT = (((1,), (1,)), ((), ()))
NN = (((1,), (0,)), ((), ()))


def dot(left, right, dims=NN):
    return lax.dot_general(left, right, dims, preferred_element_type=jnp.float32)


def split(value):
    high = value.astype(jnp.bfloat16)
    low = (value - high.astype(jnp.float32)).astype(jnp.bfloat16)
    return jnp.concatenate([high, low], axis=0)


def fold(value):
    half = value.shape[0] // 2
    return value[:half] + value[half:]


def kernel(
    n_row,
    n_col,
    columns,
    send_list,
    receive_list,
    shift_real,
    shift_imag,
    excitation_hbm,
    tiles_hbm,
    coupling_hbm,
    modes_hbm,
    inverse_hbm,
    solution_hbm,
    residual_hbm,
    solution,
    residual,
    tiles,
    coupling,
    modes,
    modes_turned,
    inverse,
    inverse_turned,
    picker,
    placer,
    field,
    base,
    gathered,
    partial,
    reduced,
    halo_out,
    halo_in,
    load_sem,
    store_sem,
    gather_send,
    gather_recv,
    reduce_send,
    reduce_recv,
    halo_send,
    halo_recv,
):
    row = lax.axis_index("row")
    col = lax.axis_index("col")
    groups, sources, _ = residual.shape
    half = sources // 2
    _, blocks, _, tile = field.shape
    per_row = tiles.shape[1]
    directions = halo_in.shape[2]
    applies = halo_in.shape[0]
    mode_count = modes_hbm.shape[0]
    padded = modes.shape[0]
    steps_per_outer = PASSES + 1

    def state_copies(source, target, sems, reverse):
        copies = []
        for g in range(groups):
            for p in range(2):
                whole = source.at[p, pl.ds(g * half, half), :]
                part = target.at[g, pl.ds(p * half, half), :]
                first, second = (part, whole) if reverse else (whole, part)
                copies.append(pltpu.make_async_copy(first, second, sems.at[2 * g + p]))
        return copies

    early = state_copies(excitation_hbm, residual, load_sem, False)
    number = len(early)
    early.append(
        pltpu.make_async_copy(modes_hbm, modes.at[pl.ds(0, mode_count), :], load_sem.at[number])
    )
    late = [
        pltpu.make_async_copy(source, target, load_sem.at[number + 1 + place])
        for place, (source, target) in enumerate(
            [(inverse_hbm, inverse), (tiles_hbm, tiles), (coupling_hbm, coupling)]
        )
    ]
    for load in early + late:
        load.start()

    barrier = pltpu.get_barrier_semaphore()
    for offset in range(1, n_row):
        pl.semaphore_signal(
            barrier, inc=1, device_id={"row": lax.rem(row + offset, n_row)}, device_id_type=MESH
        )
    for offset in range(1, n_col):
        pl.semaphore_signal(
            barrier, inc=1, device_id={"col": lax.rem(col + offset, n_col)}, device_id_type=MESH
        )

    exists = [row > 0, row < n_row - 1, col > 0, col < n_col - 1]
    target = [{"row": row - 1}, {"row": row + 1}, {"col": col - 1}, {"col": col + 1}]

    solution[...] = jnp.zeros_like(solution)
    modes[mode_count:, :] = jnp.zeros((padded - mode_count, modes.shape[1]), jnp.bfloat16)
    for d in range(directions):

        @pl.when(jnp.logical_not(exists[d]))
        def _():
            for k in range(applies):
                for g in range(groups):
                    halo_in[k, g, d] = jnp.zeros(halo_in.shape[3:], jnp.float32)

    def gather_copy(step, g, offset, slot):
        return pltpu.make_async_remote_copy(
            src_ref=gathered.at[step, g, slot],
            dst_ref=gathered.at[step, g, slot],
            send_sem=gather_send.at[step, g, offset - 1],
            recv_sem=gather_recv.at[step, g, slot],
            device_id={"row": lax.rem(row + offset, n_row)},
            device_id_type=MESH,
        )

    def reduce_copy(step, g, offset):
        peer = lax.rem(col + offset, n_col)
        return pltpu.make_async_remote_copy(
            src_ref=partial.at[step, g, peer],
            dst_ref=reduced.at[step, g, offset - 1],
            send_sem=reduce_send.at[step, g, offset - 1],
            recv_sem=reduce_recv.at[step, g, offset - 1],
            device_id={"col": peer},
            device_id_type=MESH,
        )

    def halo_copy(k, g, d, slot):
        return pltpu.make_async_remote_copy(
            src_ref=halo_out.at[k, g, d],
            dst_ref=halo_in.at[k, g, slot],
            send_sem=halo_send.at[k, g, d],
            recv_sem=halo_recv.at[k, g, slot],
            device_id=target[d],
            device_id_type=MESH,
        )

    def gather_start(step, g):
        for offset in range(1, n_row):
            gather_copy(step, g, offset, row).start()

    for load in early:
        load.wait()
    for g in range(groups):
        gathered[0, g, row] = fold(dot(split(residual[g]), modes[...], NT))
    pl.semaphore_wait(barrier, n_row - 1 + n_col - 1)
    for g in range(groups):
        gather_start(0, g)

    def prepare_first():
        late[0].wait()
        blank = jnp.zeros((padded - mode_count, inverse.shape[2]), jnp.bfloat16)

        def turn(j, carry):
            block = jnp.concatenate([inverse[j], blank], axis=0).T
            inverse_turned[:, pl.ds(pl.multiple_of(j * padded, padded), padded)] = block
            return carry

        lax.fori_loop(0, n_col, turn, 0)

    def prepare_edges():
        along = lax.broadcasted_iota(jnp.int32, (tile, tile), 1)
        down = lax.broadcasted_iota(jnp.int32, (tile, tile), 0)
        receivers = [
            jnp.broadcast_to(receive_list[d : d + 1, :], (tile, tile)).T for d in range(directions)
        ]

        def one_block(b, carry):
            start = pl.multiple_of(b * tile, tile)
            for d in range(directions):
                part = slice(d * tile, (d + 1) * tile)
                picker[pl.ds(start, tile), part] = (
                    down + start == send_list[d : d + 1, :]
                ).astype(jnp.bfloat16)
                placer[part, pl.ds(start, tile)] = (receivers[d] == along + start).astype(
                    jnp.bfloat16
                )
            return carry

        lax.fori_loop(0, blocks, one_block, 0)

    def prepare_rest():
        for load in late[1:]:
            load.wait()

        def turn(t, carry):
            for n in range(per_row):
                tiles[t, n] = tiles[t, n].T
            return carry

        lax.fori_loop(0, tiles.shape[0], turn, 0)
        for d in range(directions):
            coupling[d] = coupling[d].T
        for b in range(blocks):
            part = slice(b * tile, (b + 1) * tile)
            modes_turned[part, :] = modes[:, part].T

    def send_field(k, g, value):
        parts = split(value)
        for b in range(blocks):
            field[g, b] = parts[:, b * tile : (b + 1) * tile]
        for first in range(0, directions, 2):
            outgoing = fold(dot(parts, picker[:, first * tile : (first + 2) * tile]))
            for d in (first, first + 1):
                halo_out[k, g, d] = outgoing[:, (d - first) * tile : (d - first + 1) * tile]

                @pl.when(exists[d])
                def _():
                    halo_copy(k, g, d, d ^ 1).start()

    def coarse_product(step, g):
        for offset in range(1, n_row):
            gather_copy(step, g, offset, lax.rem(row + offset, n_row)).wait_recv()
        whole = jnp.concatenate(
            [gathered[step, g, i][:, :mode_count] for i in range(n_row)], axis=1
        )
        products = fold(dot(split(whole), inverse_turned[...]))
        for j in range(n_col):
            partial[step, g, j] = products[:, j * padded : (j + 1) * padded]
        for offset in sorted(range(1, n_col), key=lambda offset: abs(2 * offset - n_col)):
            reduce_copy(step, g, offset).start()

    def coarse_start(step, k, g):
        total = partial[step, g, col]
        for offset in range(1, n_col):
            reduce_copy(step, g, offset).wait_recv()
            total = total + reduced[step, g, offset - 1]
        start = fold(dot(split(total), modes[...]))
        send_field(k, g, start)
        solution[g] += start
        real, imag = shift_real[...], shift_imag[...]
        old = residual[g]
        base[g, :half] = old[:half] - (real * start[:half] - imag * start[half:])
        base[g, half:] = old[half:] - (real * start[half:] + imag * start[:half])

    def apply(step, sub, k, g):
        images = []
        for t in range(tiles.shape[0]):
            chosen = jnp.concatenate([field[g, columns[n, t]] for n in range(per_row)], axis=1)
            stored = tiles[t].reshape(per_row * tile, tile)
            images.append(fold(dot(chosen, stored)))
        residual[g] = base[g] - jnp.concatenate(images, axis=1)

        result = residual[g]
        for first in range(directions - 2, -1, -2):
            arrived = []
            for d in (first, first + 1):

                @pl.when(exists[d])
                def _():
                    halo_copy(k, g, d, d).wait_recv()

            for d in (first, first + 1):
                arrived.append(split(fold(dot(split(halo_in[k, g, d]), coupling[d]))))
            span = slice(first * tile, (first + 2) * tile)
            result = result - fold(dot(jnp.concatenate(arrived, axis=1), placer[span, :]))
        residual[g] = result

        @pl.when(sub < PASSES)
        def _():
            real, imag = shift_real[...], shift_imag[...]
            modulus = real * real + imag * imag
            real, imag = real / modulus, imag / modulus
            relaxed = jnp.concatenate(
                [
                    real * result[:half] + imag * result[half:],
                    real * result[half:] - imag * result[:half],
                ],
                axis=0,
            )
            send_field(k + 1, g, relaxed)
            solution[g] += relaxed
            base[g] = jnp.zeros(base.shape[1:], jnp.float32)

        @pl.when(jnp.logical_and(sub == PASSES, step < OUTER - 1))
        def _():
            gathered[step + 1, g, row] = fold(dot(split(result), modes_turned[...]))
            gather_start(step + 1, g)

    def each_group(action):
        def run(g, carry):
            action(g)
            return carry

        lax.fori_loop(0, groups, run, 0)

    def body(k, carry):
        step = lax.div(k, steps_per_outer)
        sub = lax.rem(k, steps_per_outer)

        @pl.when(k == 0)
        def _():
            prepare_first()
            prepare_edges()

        @pl.when(sub == 0)
        def _():
            each_group(lambda g: coarse_product(step, g))

        @pl.when(k == 0)
        def _():
            prepare_rest()

        @pl.when(sub == 0)
        def _():
            each_group(lambda g: coarse_start(step, k, g))

        each_group(lambda g: apply(step, sub, k, g))
        return carry

    lax.fori_loop(0, applies, body, 0)

    stores = state_copies(residual_hbm, residual, store_sem.at[0], True)
    stores += state_copies(solution_hbm, solution, store_sem.at[1], True)
    for store in stores:
        store.start()

    def finish(g):
        for step in range(OUTER):
            for offset in range(1, n_row):
                gather_copy(step, g, offset, row).wait_send()
            for offset in range(1, n_col):
                reduce_copy(step, g, offset).wait_send()
        for d in range(directions):

            @pl.when(exists[d])
            def _():
                for k in range(applies):
                    halo_copy(k, g, d, d ^ 1).wait_send()

    each_group(finish)
    for store in stores:
        store.wait()


def hand_over(first, second, first_out, second_out, sem):
    copies = []
    for place, (source, target) in enumerate([(first, first_out), (second, second_out)]):
        for p in range(source.shape[0]):
            copies.append(
                pltpu.make_async_copy(source.at[p], target.at[p], sem.at[place, p])
            )
    for copy in copies:
        copy.start()
    for copy in copies:
        copy.wait()


def on_device(
    n_row,
    n_col,
    excitation,
    shift_real,
    shift_imag,
    local_tiles,
    tile_columns,
    coupling,
    send_edges,
    receive_edges,
    local_modes,
    coarse_inverse,
):
    shape = excitation.shape
    edges = shape[-1]
    sources = shape[2] * shape[3] // GROUPS
    tile_rows, per_row, tile, _ = local_tiles.shape[2:]
    directions = send_edges.shape[2]
    mode_count = local_modes.shape[2]
    padded = -(-mode_count // tile) * tile
    applies = OUTER * (PASSES + 1)
    vmem = pl.BlockSpec(memory_space=pltpu.VMEM)
    hbm = pl.BlockSpec(memory_space=pl.ANY)
    flat = jax.ShapeDtypeStruct(shape[2:], jnp.float32)
    state = pltpu.VMEM((GROUPS, sources, edges), jnp.float32)
    halo = pltpu.VMEM((applies, GROUPS, directions, sources, tile), jnp.float32)
    inverse = coarse_inverse.reshape(n_col, mode_count, coarse_inverse.shape[1])
    results = pl.pallas_call(
        functools.partial(kernel, n_row, n_col),
        out_shape=(flat, flat),
        in_specs=[pl.BlockSpec(memory_space=pltpu.SMEM)] + [vmem] * 4 + [hbm] * 5,
        out_specs=(hbm, hbm),
        scratch_shapes=[
            state,
            state,
            pltpu.VMEM(local_tiles.shape[2:], jnp.bfloat16),
            pltpu.VMEM(coupling.shape[2:], jnp.bfloat16),
            pltpu.VMEM((padded, edges), jnp.bfloat16),
            pltpu.VMEM((edges, padded), jnp.bfloat16),
            pltpu.VMEM(inverse.shape, jnp.bfloat16),
            pltpu.VMEM((inverse.shape[2], n_col * padded), jnp.bfloat16),
            pltpu.VMEM((edges, directions * tile), jnp.bfloat16),
            pltpu.VMEM((directions * tile, edges), jnp.bfloat16),
            pltpu.VMEM((GROUPS, edges // tile, 2 * sources, tile), jnp.bfloat16),
            state,
            pltpu.VMEM((OUTER, GROUPS, n_row, sources, padded), jnp.float32),
            pltpu.VMEM((OUTER, GROUPS, n_col, sources, padded), jnp.float32),
            pltpu.VMEM((OUTER, GROUPS, n_col - 1, sources, padded), jnp.float32),
            halo,
            halo,
            pltpu.SemaphoreType.DMA((2 * GROUPS + 4,)),
            pltpu.SemaphoreType.DMA((2, 2 * GROUPS)),
            pltpu.SemaphoreType.DMA((OUTER, GROUPS, n_row - 1)),
            pltpu.SemaphoreType.DMA((OUTER, GROUPS, n_row)),
            pltpu.SemaphoreType.DMA((OUTER, GROUPS, n_col - 1)),
            pltpu.SemaphoreType.DMA((OUTER, GROUPS, n_col - 1)),
            pltpu.SemaphoreType.DMA((applies, GROUPS, directions)),
            pltpu.SemaphoreType.DMA((applies, GROUPS, directions)),
        ],
        compiler_params=pltpu.CompilerParams(
            collective_id=0, has_side_effects=True, vmem_limit_bytes=63 * 1024 * 1024
        ),
    )(
        tile_columns[0, 0].T,
        send_edges[0, 0],
        receive_edges[0, 0],
        shift_real[0],
        shift_imag[0],
        excitation[0, 0],
        local_tiles[0, 0],
        coupling[0, 0],
        local_modes[0, 0],
        inverse,
    )
    results = pl.pallas_call(
        hand_over,
        out_shape=(flat, flat),
        in_specs=[hbm, hbm],
        out_specs=(hbm, hbm),
        scratch_shapes=[pltpu.SemaphoreType.DMA((2, shape[2]))],
        compiler_params=pltpu.CompilerParams(vmem_limit_bytes=63 * 1024 * 1024),
    )(*results)
    return tuple(value.reshape(shape) for value in results)


def solution(mesh):
    in_specs = (
        P("row", "col", None, None, None),
        P("row", "col", None),
        P("row", "col", None),
        P("row", "col", None, None, None, None),
        P("row", "col", None, None),
        P("row", "col", None, None, None),
        P("row", "col", None, None),
        P("row", "col", None, None),
        P("row", "col", None, None),
        P("row", "col"),
    )
    out_specs = (P("row", "col", None, None, None), P("row", "col", None, None, None))
    return jax.shard_map(
        functools.partial(on_device, mesh.shape["row"], mesh.shape["col"]),
        mesh=mesh,
        in_specs=in_specs,
        out_specs=out_specs,
        check_vma=False,
    )
```

```python
import functools

import jax
import jax.numpy as jnp
from jax import lax
from jax.experimental import pallas as pl
from jax.experimental.pallas import tpu as pltpu
from jax.sharding import PartitionSpec as P

OUTER = 2
PASSES = 2
GROUPS = 1
MESH = pl.DeviceIdType.MESH
NT = (((1,), (1,)), ((), ()))
NN = (((1,), (0,)), ((), ()))


def dot(left, right, dims=NN):
    return lax.dot_general(left, right, dims, preferred_element_type=jnp.float32)


def split(value):
    high = value.astype(jnp.bfloat16)
    low = (value - high.astype(jnp.float32)).astype(jnp.bfloat16)
    return jnp.concatenate([high, low], axis=0)


def fold(value):
    half = value.shape[0] // 2
    return value[:half] + value[half:]


def kernel(
    n_row,
    n_col,
    columns,
    send_list,
    receive_list,
    shift_real,
    shift_imag,
    excitation_hbm,
    tiles_hbm,
    coupling_hbm,
    modes_hbm,
    inverse_hbm,
    solution_hbm,
    residual_hbm,
    solution,
    residual,
    tiles,
    coupling,
    modes,
    modes_turned,
    inverse,
    inverse_turned,
    picker,
    placer,
    field,
    base,
    gathered,
    partial,
    reduced,
    halo_out,
    halo_in,
    load_sem,
    store_sem,
    gather_send,
    gather_recv,
    reduce_send,
    reduce_recv,
    halo_send,
    halo_recv,
):
    row = lax.axis_index("row")
    col = lax.axis_index("col")
    groups, sources, _ = residual.shape
    half = sources // 2
    _, blocks, _, tile = field.shape
    per_row = tiles.shape[1]
    directions = halo_in.shape[2]
    applies = halo_in.shape[0]
    mode_count = modes_hbm.shape[0]
    padded = modes.shape[0]
    steps_per_outer = PASSES + 1

    def state_copies(source, target, sems, reverse):
        copies = []
        for g in range(groups):
            for p in range(2):
                whole = source.at[p, pl.ds(g * half, half), :]
                part = target.at[g, pl.ds(p * half, half), :]
                first, second = (part, whole) if reverse else (whole, part)
                copies.append(pltpu.make_async_copy(first, second, sems.at[2 * g + p]))
        return copies

    early = state_copies(excitation_hbm, residual, load_sem, False)
    number = len(early)
    early.append(
        pltpu.make_async_copy(modes_hbm, modes.at[pl.ds(0, mode_count), :], load_sem.at[number])
    )
    late = [
        pltpu.make_async_copy(source, target, load_sem.at[number + 1 + place])
        for place, (source, target) in enumerate(
            [(inverse_hbm, inverse), (tiles_hbm, tiles), (coupling_hbm, coupling)]
        )
    ]
    for load in early + late:
        load.start()

    barrier = pltpu.get_barrier_semaphore()
    for offset in range(1, n_row):
        pl.semaphore_signal(
            barrier, inc=1, device_id={"row": lax.rem(row + offset, n_row)}, device_id_type=MESH
        )
    for offset in range(1, n_col):
        pl.semaphore_signal(
            barrier, inc=1, device_id={"col": lax.rem(col + offset, n_col)}, device_id_type=MESH
        )

    exists = [row > 0, row < n_row - 1, col > 0, col < n_col - 1]
    target = [{"row": row - 1}, {"row": row + 1}, {"col": col - 1}, {"col": col + 1}]

    solution[...] = jnp.zeros_like(solution)
    modes[mode_count:, :] = jnp.zeros((padded - mode_count, modes.shape[1]), jnp.bfloat16)
    for d in range(directions):

        @pl.when(jnp.logical_not(exists[d]))
        def _():
            for k in range(applies):
                for g in range(groups):
                    halo_in[k, g, d] = jnp.zeros(halo_in.shape[3:], jnp.float32)

    def gather_copy(step, g, offset, slot):
        return pltpu.make_async_remote_copy(
            src_ref=gathered.at[step, g, slot],
            dst_ref=gathered.at[step, g, slot],
            send_sem=gather_send.at[step, g, offset - 1],
            recv_sem=gather_recv.at[step, g, slot],
            device_id={"row": lax.rem(row + offset, n_row)},
            device_id_type=MESH,
        )

    def reduce_copy(step, g, offset):
        peer = lax.rem(col + offset, n_col)
        return pltpu.make_async_remote_copy(
            src_ref=partial.at[step, g, peer],
            dst_ref=reduced.at[step, g, offset - 1],
            send_sem=reduce_send.at[step, g, offset - 1],
            recv_sem=reduce_recv.at[step, g, offset - 1],
            device_id={"col": peer},
            device_id_type=MESH,
        )

    def halo_copy(k, g, d, slot):
        return pltpu.make_async_remote_copy(
            src_ref=halo_out.at[k, g, d],
            dst_ref=halo_in.at[k, g, slot],
            send_sem=halo_send.at[k, g, d],
            recv_sem=halo_recv.at[k, g, slot],
            device_id=target[d],
            device_id_type=MESH,
        )

    def gather_start(step, g):
        for offset in range(1, n_row):
            gather_copy(step, g, offset, row).start()

    for load in early:
        load.wait()
    for g in range(groups):
        gathered[0, g, row] = fold(dot(split(residual[g]), modes[...], NT))
    pl.semaphore_wait(barrier, n_row - 1 + n_col - 1)
    for g in range(groups):
        gather_start(0, g)

    def prepare_first():
        late[0].wait()
        blank = jnp.zeros((padded - mode_count, inverse.shape[2]), jnp.bfloat16)

        def turn(j, carry):
            block = jnp.concatenate([inverse[j], blank], axis=0).T
            inverse_turned[:, pl.ds(pl.multiple_of(j * padded, padded), padded)] = block
            return carry

        lax.fori_loop(0, n_col, turn, 0)

    def prepare_edges():
        along = lax.broadcasted_iota(jnp.int32, (tile, tile), 1)
        down = lax.broadcasted_iota(jnp.int32, (tile, tile), 0)
        receivers = [
            jnp.broadcast_to(receive_list[d : d + 1, :], (tile, tile)).T for d in range(directions)
        ]

        def one_block(b, carry):
            start = pl.multiple_of(b * tile, tile)
            for d in range(directions):
                part = slice(d * tile, (d + 1) * tile)
                picker[pl.ds(start, tile), part] = (
                    down + start == send_list[d : d + 1, :]
                ).astype(jnp.bfloat16)
                placer[part, pl.ds(start, tile)] = (receivers[d] == along + start).astype(
                    jnp.bfloat16
                )
            return carry

        lax.fori_loop(0, blocks, one_block, 0)

    def prepare_rest():
        for load in late[1:]:
            load.wait()

        def turn(t, carry):
            for n in range(per_row):
                tiles[t, n] = tiles[t, n].T
            return carry

        lax.fori_loop(0, tiles.shape[0], turn, 0)
        for d in range(directions):
            coupling[d] = coupling[d].T
        for b in range(blocks):
            part = slice(b * tile, (b + 1) * tile)
            modes_turned[part, :] = modes[:, part].T

    def send_field(k, g, value):
        parts = split(value)
        for b in range(blocks):
            field[g, b] = parts[:, b * tile : (b + 1) * tile]
        for first in range(0, directions, 2):
            outgoing = fold(dot(parts, picker[:, first * tile : (first + 2) * tile]))
            for d in (first, first + 1):
                halo_out[k, g, d] = outgoing[:, (d - first) * tile : (d - first + 1) * tile]

                @pl.when(exists[d])
                def _():
                    halo_copy(k, g, d, d ^ 1).start()

    def coarse_product(step, g):
        for offset in range(1, n_row):
            gather_copy(step, g, offset, lax.rem(row + offset, n_row)).wait_recv()
        whole = jnp.concatenate(
            [gathered[step, g, i][:, :mode_count] for i in range(n_row)], axis=1
        )
        products = fold(dot(split(whole), inverse_turned[...]))
        for j in range(n_col):
            partial[step, g, j] = products[:, j * padded : (j + 1) * padded]
        for offset in sorted(range(1, n_col), key=lambda offset: abs(2 * offset - n_col)):
            reduce_copy(step, g, offset).start()

    def coarse_start(step, k, g):
        total = partial[step, g, col]
        for offset in range(1, n_col):
            reduce_copy(step, g, offset).wait_recv()
            total = total + reduced[step, g, offset - 1]
        start = fold(dot(split(total), modes[...]))
        send_field(k, g, start)
        solution[g] += start
        real, imag = shift_real[...], shift_imag[...]
        old = residual[g]
        base[g, :half] = old[:half] - (real * start[:half] - imag * start[half:])
        base[g, half:] = old[half:] - (real * start[half:] + imag * start[:half])

    def apply(step, sub, k, g):
        images = []
        for t in range(tiles.shape[0]):
            chosen = jnp.concatenate([field[g, columns[n, t]] for n in range(per_row)], axis=1)
            stored = tiles[t].reshape(per_row * tile, tile)
            images.append(fold(dot(chosen, stored)))
        residual[g] = base[g] - jnp.concatenate(images, axis=1)

        result = residual[g]
        for first in range(directions - 2, -1, -2):
            arrived = []
            for d in (first, first + 1):

                @pl.when(exists[d])
                def _():
                    halo_copy(k, g, d, d).wait_recv()

            for d in (first, first + 1):
                arrived.append(split(fold(dot(split(halo_in[k, g, d]), coupling[d]))))
            span = slice(first * tile, (first + 2) * tile)
            result = result - fold(dot(jnp.concatenate(arrived, axis=1), placer[span, :]))
        residual[g] = result

        @pl.when(sub < PASSES)
        def _():
            real, imag = shift_real[...], shift_imag[...]
            modulus = real * real + imag * imag
            real, imag = real / modulus, imag / modulus
            relaxed = jnp.concatenate(
                [
                    real * result[:half] + imag * result[half:],
                    real * result[half:] - imag * result[:half],
                ],
                axis=0,
            )
            send_field(k + 1, g, relaxed)
            solution[g] += relaxed
            base[g] = jnp.zeros(base.shape[1:], jnp.float32)

        @pl.when(jnp.logical_and(sub == PASSES, step < OUTER - 1))
        def _():
            gathered[step + 1, g, row] = fold(dot(split(result), modes_turned[...]))
            gather_start(step + 1, g)

    def each_group(action):
        def run(g, carry):
            action(g)
            return carry

        lax.fori_loop(0, groups, run, 0)

    def body(k, carry):
        step = lax.div(k, steps_per_outer)
        sub = lax.rem(k, steps_per_outer)

        @pl.when(k == 0)
        def _():
            prepare_first()
            prepare_edges()

        @pl.when(sub == 0)
        def _():
            each_group(lambda g: coarse_product(step, g))

        @pl.when(k == 0)
        def _():
            prepare_rest()

        @pl.when(sub == 0)
        def _():
            each_group(lambda g: coarse_start(step, k, g))

        each_group(lambda g: apply(step, sub, k, g))
        return carry

    lax.fori_loop(0, applies, body, 0)

    stores = state_copies(residual_hbm, residual, store_sem.at[0], True)
    stores += state_copies(solution_hbm, solution, store_sem.at[1], True)
    for store in stores:
        store.start()

    def finish(g):
        for step in range(OUTER):
            for offset in range(1, n_row):
                gather_copy(step, g, offset, row).wait_send()
            for offset in range(1, n_col):
                reduce_copy(step, g, offset).wait_send()
        for d in range(directions):

            @pl.when(exists[d])
            def _():
                for k in range(applies):
                    halo_copy(k, g, d, d ^ 1).wait_send()

    each_group(finish)
    for store in stores:
        store.wait()


def hand_over(first, second, first_out, second_out, held, arrive_sem, leave_sem):
    arrivals, departures = [], []
    for place, (source, target) in enumerate([(first, first_out), (second, second_out)]):
        for p in range(source.shape[0]):
            slot = held.at[place, p]
            arrivals.append(
                pltpu.make_async_copy(source.at[p], slot, arrive_sem.at[place, p])
            )
            departures.append(
                pltpu.make_async_copy(slot, target.at[p], leave_sem.at[place, p])
            )
    for arrival in arrivals:
        arrival.start()
    for arrival, departure in zip(arrivals, departures):
        arrival.wait()
        departure.start()
    for departure in departures:
        departure.wait()


def on_device(
    n_row,
    n_col,
    excitation,
    shift_real,
    shift_imag,
    local_tiles,
    tile_columns,
    coupling,
    send_edges,
    receive_edges,
    local_modes,
    coarse_inverse,
):
    shape = excitation.shape
    edges = shape[-1]
    sources = shape[2] * shape[3] // GROUPS
    tile_rows, per_row, tile, _ = local_tiles.shape[2:]
    directions = send_edges.shape[2]
    mode_count = local_modes.shape[2]
    padded = -(-mode_count // tile) * tile
    applies = OUTER * (PASSES + 1)
    vmem = pl.BlockSpec(memory_space=pltpu.VMEM)
    hbm = pl.BlockSpec(memory_space=pl.ANY)
    flat = jax.ShapeDtypeStruct(shape[2:], jnp.float32)
    state = pltpu.VMEM((GROUPS, sources, edges), jnp.float32)
    halo = pltpu.VMEM((applies, GROUPS, directions, sources, tile), jnp.float32)
    inverse = coarse_inverse.reshape(n_col, mode_count, coarse_inverse.shape[1])
    results = pl.pallas_call(
        functools.partial(kernel, n_row, n_col),
        out_shape=(flat, flat),
        in_specs=[pl.BlockSpec(memory_space=pltpu.SMEM)] + [vmem] * 4 + [hbm] * 5,
        out_specs=(hbm, hbm),
        scratch_shapes=[
            state,
            state,
            pltpu.VMEM(local_tiles.shape[2:], jnp.bfloat16),
            pltpu.VMEM(coupling.shape[2:], jnp.bfloat16),
            pltpu.VMEM((padded, edges), jnp.bfloat16),
            pltpu.VMEM((edges, padded), jnp.bfloat16),
            pltpu.VMEM(inverse.shape, jnp.bfloat16),
            pltpu.VMEM((inverse.shape[2], n_col * padded), jnp.bfloat16),
            pltpu.VMEM((edges, directions * tile), jnp.bfloat16),
            pltpu.VMEM((directions * tile, edges), jnp.bfloat16),
            pltpu.VMEM((GROUPS, edges // tile, 2 * sources, tile), jnp.bfloat16),
            state,
            pltpu.VMEM((OUTER, GROUPS, n_row, sources, padded), jnp.float32),
            pltpu.VMEM((OUTER, GROUPS, n_col, sources, padded), jnp.float32),
            pltpu.VMEM((OUTER, GROUPS, n_col - 1, sources, padded), jnp.float32),
            halo,
            halo,
            pltpu.SemaphoreType.DMA((2 * GROUPS + 4,)),
            pltpu.SemaphoreType.DMA((2, 2 * GROUPS)),
            pltpu.SemaphoreType.DMA((OUTER, GROUPS, n_row - 1)),
            pltpu.SemaphoreType.DMA((OUTER, GROUPS, n_row)),
            pltpu.SemaphoreType.DMA((OUTER, GROUPS, n_col - 1)),
            pltpu.SemaphoreType.DMA((OUTER, GROUPS, n_col - 1)),
            pltpu.SemaphoreType.DMA((applies, GROUPS, directions)),
            pltpu.SemaphoreType.DMA((applies, GROUPS, directions)),
        ],
        compiler_params=pltpu.CompilerParams(
            collective_id=0, has_side_effects=True, vmem_limit_bytes=63 * 1024 * 1024
        ),
    )(
        tile_columns[0, 0].T,
        send_edges[0, 0],
        receive_edges[0, 0],
        shift_real[0],
        shift_imag[0],
        excitation[0, 0],
        local_tiles[0, 0],
        coupling[0, 0],
        local_modes[0, 0],
        inverse,
    )
    results = pl.pallas_call(
        hand_over,
        out_shape=(flat, flat),
        in_specs=[hbm, hbm],
        out_specs=(hbm, hbm),
        scratch_shapes=[
            pltpu.VMEM((2,) + shape[2:], jnp.float32),
            pltpu.SemaphoreType.DMA((2, shape[2])),
            pltpu.SemaphoreType.DMA((2, shape[2])),
        ],
        compiler_params=pltpu.CompilerParams(vmem_limit_bytes=63 * 1024 * 1024),
    )(*results)
    return tuple(value.reshape(shape) for value in results)


def solution(mesh):
    in_specs = (
        P("row", "col", None, None, None),
        P("row", "col", None),
        P("row", "col", None),
        P("row", "col", None, None, None, None),
        P("row", "col", None, None),
        P("row", "col", None, None, None),
        P("row", "col", None, None),
        P("row", "col", None, None),
        P("row", "col", None, None),
        P("row", "col"),
    )
    out_specs = (P("row", "col", None, None, None), P("row", "col", None, None, None))
    return jax.shard_map(
        functools.partial(on_device, mesh.shape["row"], mesh.shape["col"]),
        mesh=mesh,
        in_specs=in_specs,
        out_specs=out_specs,
        check_vma=False,
    )
```

```python
import functools

import jax
import jax.numpy as jnp
from jax import lax
from jax.experimental import pallas as pl
from jax.experimental.pallas import tpu as pltpu
from jax.sharding import PartitionSpec as P

OUTER = 2
PASSES = 2
GROUPS = 2
MESH = pl.DeviceIdType.MESH
NT = (((1,), (1,)), ((), ()))
NN = (((1,), (0,)), ((), ()))


def dot(left, right, dims=NN):
    return lax.dot_general(left, right, dims, preferred_element_type=jnp.float32)


def split(value):
    high = value.astype(jnp.bfloat16)
    low = (value - high.astype(jnp.float32)).astype(jnp.bfloat16)
    return jnp.concatenate([high, low], axis=0)


def fold(value):
    half = value.shape[0] // 2
    return value[:half] + value[half:]


def kernel(
    n_row,
    n_col,
    columns,
    send_list,
    receive_list,
    shift_real,
    shift_imag,
    excitation_hbm,
    tiles_hbm,
    coupling_hbm,
    modes_hbm,
    inverse_hbm,
    solution_hbm,
    residual_hbm,
    solution,
    residual,
    tiles,
    coupling,
    modes,
    modes_turned,
    inverse,
    inverse_turned,
    picker,
    placer,
    field,
    base,
    gathered,
    partial,
    reduced,
    halo_out,
    halo_in,
    load_sem,
    store_sem,
    gather_send,
    gather_recv,
    reduce_send,
    reduce_recv,
    halo_send,
    halo_recv,
):
    row = lax.axis_index("row")
    col = lax.axis_index("col")
    groups, sources, _ = residual.shape
    half = sources // 2
    _, blocks, _, tile = field.shape
    per_row = tiles.shape[1]
    directions = halo_in.shape[2]
    applies = halo_in.shape[0]
    mode_count = modes_hbm.shape[0]
    padded = modes.shape[0]
    steps_per_outer = PASSES + 1

    def state_copies(source, target, sems, reverse):
        copies = []
        for g in range(groups):
            for p in range(2):
                whole = source.at[p, pl.ds(g * half, half), :]
                part = target.at[g, pl.ds(p * half, half), :]
                first, second = (part, whole) if reverse else (whole, part)
                copies.append(pltpu.make_async_copy(first, second, sems.at[2 * g + p]))
        return copies

    early = state_copies(excitation_hbm, residual, load_sem, False)
    number = len(early)
    early.append(
        pltpu.make_async_copy(modes_hbm, modes.at[pl.ds(0, mode_count), :], load_sem.at[number])
    )
    late = [
        pltpu.make_async_copy(source, target, load_sem.at[number + 1 + place])
        for place, (source, target) in enumerate(
            [(inverse_hbm, inverse), (tiles_hbm, tiles), (coupling_hbm, coupling)]
        )
    ]
    for load in early + late:
        load.start()

    barrier = pltpu.get_barrier_semaphore()
    for offset in range(1, n_row):
        pl.semaphore_signal(
            barrier, inc=1, device_id={"row": lax.rem(row + offset, n_row)}, device_id_type=MESH
        )
    for offset in range(1, n_col):
        pl.semaphore_signal(
            barrier, inc=1, device_id={"col": lax.rem(col + offset, n_col)}, device_id_type=MESH
        )

    exists = [row > 0, row < n_row - 1, col > 0, col < n_col - 1]
    target = [{"row": row - 1}, {"row": row + 1}, {"col": col - 1}, {"col": col + 1}]

    solution[...] = jnp.zeros_like(solution)
    modes[mode_count:, :] = jnp.zeros((padded - mode_count, modes.shape[1]), jnp.bfloat16)
    for d in range(directions):

        @pl.when(jnp.logical_not(exists[d]))
        def _():
            for k in range(applies):
                for g in range(groups):
                    halo_in[k, g, d] = jnp.zeros(halo_in.shape[3:], jnp.float32)

    def gather_copy(step, g, offset, slot):
        return pltpu.make_async_remote_copy(
            src_ref=gathered.at[step, g, slot],
            dst_ref=gathered.at[step, g, slot],
            send_sem=gather_send.at[step, g, offset - 1],
            recv_sem=gather_recv.at[step, g, slot],
            device_id={"row": lax.rem(row + offset, n_row)},
            device_id_type=MESH,
        )

    def reduce_copy(step, g, offset):
        peer = lax.rem(col + offset, n_col)
        return pltpu.make_async_remote_copy(
            src_ref=partial.at[step, g, peer],
            dst_ref=reduced.at[step, g, offset - 1],
            send_sem=reduce_send.at[step, g, offset - 1],
            recv_sem=reduce_recv.at[step, g, offset - 1],
            device_id={"col": peer},
            device_id_type=MESH,
        )

    def halo_copy(k, g, d, slot):
        return pltpu.make_async_remote_copy(
            src_ref=halo_out.at[k, g, d],
            dst_ref=halo_in.at[k, g, slot],
            send_sem=halo_send.at[k, g, d],
            recv_sem=halo_recv.at[k, g, slot],
            device_id=target[d],
            device_id_type=MESH,
        )

    def gather_start(step, g):
        for offset in range(1, n_row):
            gather_copy(step, g, offset, row).start()

    for load in early:
        load.wait()
    for g in range(groups):
        gathered[0, g, row] = fold(dot(split(residual[g]), modes[...], NT))
    pl.semaphore_wait(barrier, n_row - 1 + n_col - 1)
    for g in range(groups):
        gather_start(0, g)

    def prepare_first():
        late[0].wait()
        blank = jnp.zeros((padded - mode_count, inverse.shape[2]), jnp.bfloat16)

        def turn(j, carry):
            block = jnp.concatenate([inverse[j], blank], axis=0).T
            inverse_turned[:, pl.ds(pl.multiple_of(j * padded, padded), padded)] = block
            return carry

        lax.fori_loop(0, n_col, turn, 0)

    def prepare_edges():
        along = lax.broadcasted_iota(jnp.int32, (tile, tile), 1)
        down = lax.broadcasted_iota(jnp.int32, (tile, tile), 0)
        receivers = [
            jnp.broadcast_to(receive_list[d : d + 1, :], (tile, tile)).T for d in range(directions)
        ]

        def one_block(b, carry):
            start = pl.multiple_of(b * tile, tile)
            for d in range(directions):
                part = slice(d * tile, (d + 1) * tile)
                picker[pl.ds(start, tile), part] = (
                    down + start == send_list[d : d + 1, :]
                ).astype(jnp.bfloat16)
                placer[part, pl.ds(start, tile)] = (receivers[d] == along + start).astype(
                    jnp.bfloat16
                )
            return carry

        lax.fori_loop(0, blocks, one_block, 0)

    def prepare_rest():
        for load in late[1:]:
            load.wait()

        def turn(t, carry):
            for n in range(per_row):
                tiles[t, n] = tiles[t, n].T
            return carry

        lax.fori_loop(0, tiles.shape[0], turn, 0)
        for d in range(directions):
            coupling[d] = coupling[d].T
        for b in range(blocks):
            part = slice(b * tile, (b + 1) * tile)
            modes_turned[part, :] = modes[:, part].T

    def send_field(k, g, value):
        parts = split(value)
        for b in range(blocks):
            field[g, b] = parts[:, b * tile : (b + 1) * tile]
        for first in range(0, directions, 2):
            outgoing = fold(dot(parts, picker[:, first * tile : (first + 2) * tile]))
            for d in (first, first + 1):
                halo_out[k, g, d] = outgoing[:, (d - first) * tile : (d - first + 1) * tile]

                @pl.when(exists[d])
                def _():
                    halo_copy(k, g, d, d ^ 1).start()

    def coarse_product(step, g):
        for offset in range(1, n_row):
            gather_copy(step, g, offset, lax.rem(row + offset, n_row)).wait_recv()
        whole = jnp.concatenate(
            [gathered[step, g, i][:, :mode_count] for i in range(n_row)], axis=1
        )
        products = fold(dot(split(whole), inverse_turned[...]))
        for j in range(n_col):
            partial[step, g, j] = products[:, j * padded : (j + 1) * padded]
        for offset in sorted(range(1, n_col), key=lambda offset: abs(2 * offset - n_col)):
            reduce_copy(step, g, offset).start()

    def coarse_start(step, k, g):
        total = partial[step, g, col]
        for offset in range(1, n_col):
            reduce_copy(step, g, offset).wait_recv()
            total = total + reduced[step, g, offset - 1]
        start = fold(dot(split(total), modes[...]))
        send_field(k, g, start)
        solution[g] += start
        real, imag = shift_real[...], shift_imag[...]
        old = residual[g]
        base[g, :half] = old[:half] - (real * start[:half] - imag * start[half:])
        base[g, half:] = old[half:] - (real * start[half:] + imag * start[:half])

    def apply(step, sub, k, g):
        images = []
        for t in range(tiles.shape[0]):
            chosen = jnp.concatenate([field[g, columns[n, t]] for n in range(per_row)], axis=1)
            stored = tiles[t].reshape(per_row * tile, tile)
            images.append(fold(dot(chosen, stored)))
        residual[g] = base[g] - jnp.concatenate(images, axis=1)

        result = residual[g]
        for first in range(directions - 2, -1, -2):
            arrived = []
            for d in (first, first + 1):

                @pl.when(exists[d])
                def _():
                    halo_copy(k, g, d, d).wait_recv()

            for d in (first, first + 1):
                arrived.append(split(fold(dot(split(halo_in[k, g, d]), coupling[d]))))
            span = slice(first * tile, (first + 2) * tile)
            result = result - fold(dot(jnp.concatenate(arrived, axis=1), placer[span, :]))
        residual[g] = result

        @pl.when(sub < PASSES)
        def _():
            real, imag = shift_real[...], shift_imag[...]
            modulus = real * real + imag * imag
            real, imag = real / modulus, imag / modulus
            relaxed = jnp.concatenate(
                [
                    real * result[:half] + imag * result[half:],
                    real * result[half:] - imag * result[:half],
                ],
                axis=0,
            )
            send_field(k + 1, g, relaxed)
            solution[g] += relaxed
            base[g] = jnp.zeros(base.shape[1:], jnp.float32)

        @pl.when(jnp.logical_and(sub == PASSES, step < OUTER - 1))
        def _():
            gathered[step + 1, g, row] = fold(dot(split(result), modes_turned[...]))
            gather_start(step + 1, g)

    def each_group(action):
        def run(g, carry):
            action(g)
            return carry

        lax.fori_loop(0, groups, run, 0)

    def body(k, carry):
        step = lax.div(k, steps_per_outer)
        sub = lax.rem(k, steps_per_outer)

        @pl.when(k == 0)
        def _():
            prepare_first()
            prepare_edges()

        @pl.when(sub == 0)
        def _():
            each_group(lambda g: coarse_product(step, g))

        @pl.when(k == 0)
        def _():
            prepare_rest()

        @pl.when(sub == 0)
        def _():
            each_group(lambda g: coarse_start(step, k, g))

        each_group(lambda g: apply(step, sub, k, g))
        return carry

    lax.fori_loop(0, applies, body, 0)

    stores = state_copies(residual_hbm, residual, store_sem.at[0], True)
    stores += state_copies(solution_hbm, solution, store_sem.at[1], True)
    for store in stores:
        store.start()

    def finish(g):
        for step in range(OUTER):
            for offset in range(1, n_row):
                gather_copy(step, g, offset, row).wait_send()
            for offset in range(1, n_col):
                reduce_copy(step, g, offset).wait_send()
        for d in range(directions):

            @pl.when(exists[d])
            def _():
                for k in range(applies):
                    halo_copy(k, g, d, d ^ 1).wait_send()

    each_group(finish)
    for store in stores:
        store.wait()


def hand_over(first, second, first_out, second_out, held, arrive_sem, leave_sem):
    arrivals, departures = [], []
    for place, (source, target) in enumerate([(first, first_out), (second, second_out)]):
        for p in range(source.shape[0]):
            slot = held.at[place, p]
            arrivals.append(
                pltpu.make_async_copy(source.at[p], slot, arrive_sem.at[place, p])
            )
            departures.append(
                pltpu.make_async_copy(slot, target.at[p], leave_sem.at[place, p])
            )
    for arrival in arrivals:
        arrival.start()
    for arrival, departure in zip(arrivals, departures):
        arrival.wait()
        departure.start()
    for departure in departures:
        departure.wait()


def on_device(
    n_row,
    n_col,
    excitation,
    shift_real,
    shift_imag,
    local_tiles,
    tile_columns,
    coupling,
    send_edges,
    receive_edges,
    local_modes,
    coarse_inverse,
):
    shape = excitation.shape
    edges = shape[-1]
    sources = shape[2] * shape[3] // GROUPS
    tile_rows, per_row, tile, _ = local_tiles.shape[2:]
    directions = send_edges.shape[2]
    mode_count = local_modes.shape[2]
    padded = -(-mode_count // tile) * tile
    applies = OUTER * (PASSES + 1)
    vmem = pl.BlockSpec(memory_space=pltpu.VMEM)
    hbm = pl.BlockSpec(memory_space=pl.ANY)
    flat = jax.ShapeDtypeStruct(shape[2:], jnp.float32)
    state = pltpu.VMEM((GROUPS, sources, edges), jnp.float32)
    halo = pltpu.VMEM((applies, GROUPS, directions, sources, tile), jnp.float32)
    inverse = coarse_inverse.reshape(n_col, mode_count, coarse_inverse.shape[1])
    results = pl.pallas_call(
        functools.partial(kernel, n_row, n_col),
        out_shape=(flat, flat),
        in_specs=[pl.BlockSpec(memory_space=pltpu.SMEM)] + [vmem] * 4 + [hbm] * 5,
        out_specs=(hbm, hbm),
        scratch_shapes=[
            state,
            state,
            pltpu.VMEM(local_tiles.shape[2:], jnp.bfloat16),
            pltpu.VMEM(coupling.shape[2:], jnp.bfloat16),
            pltpu.VMEM((padded, edges), jnp.bfloat16),
            pltpu.VMEM((edges, padded), jnp.bfloat16),
            pltpu.VMEM(inverse.shape, jnp.bfloat16),
            pltpu.VMEM((inverse.shape[2], n_col * padded), jnp.bfloat16),
            pltpu.VMEM((edges, directions * tile), jnp.bfloat16),
            pltpu.VMEM((directions * tile, edges), jnp.bfloat16),
            pltpu.VMEM((GROUPS, edges // tile, 2 * sources, tile), jnp.bfloat16),
            state,
            pltpu.VMEM((OUTER, GROUPS, n_row, sources, padded), jnp.float32),
            pltpu.VMEM((OUTER, GROUPS, n_col, sources, padded), jnp.float32),
            pltpu.VMEM((OUTER, GROUPS, n_col - 1, sources, padded), jnp.float32),
            halo,
            halo,
            pltpu.SemaphoreType.DMA((2 * GROUPS + 4,)),
            pltpu.SemaphoreType.DMA((2, 2 * GROUPS)),
            pltpu.SemaphoreType.DMA((OUTER, GROUPS, n_row - 1)),
            pltpu.SemaphoreType.DMA((OUTER, GROUPS, n_row)),
            pltpu.SemaphoreType.DMA((OUTER, GROUPS, n_col - 1)),
            pltpu.SemaphoreType.DMA((OUTER, GROUPS, n_col - 1)),
            pltpu.SemaphoreType.DMA((applies, GROUPS, directions)),
            pltpu.SemaphoreType.DMA((applies, GROUPS, directions)),
        ],
        compiler_params=pltpu.CompilerParams(
            collective_id=0, has_side_effects=True, vmem_limit_bytes=63 * 1024 * 1024
        ),
    )(
        tile_columns[0, 0].T,
        send_edges[0, 0],
        receive_edges[0, 0],
        shift_real[0],
        shift_imag[0],
        excitation[0, 0],
        local_tiles[0, 0],
        coupling[0, 0],
        local_modes[0, 0],
        inverse,
    )
    results = pl.pallas_call(
        hand_over,
        out_shape=(flat, flat),
        in_specs=[hbm, hbm],
        out_specs=(hbm, hbm),
        scratch_shapes=[
            pltpu.VMEM((2,) + shape[2:], jnp.float32),
            pltpu.SemaphoreType.DMA((2, shape[2])),
            pltpu.SemaphoreType.DMA((2, shape[2])),
        ],
        compiler_params=pltpu.CompilerParams(vmem_limit_bytes=63 * 1024 * 1024),
    )(*results)
    return tuple(value.reshape(shape) for value in results)


def solution(mesh):
    in_specs = (
        P("row", "col", None, None, None),
        P("row", "col", None),
        P("row", "col", None),
        P("row", "col", None, None, None, None),
        P("row", "col", None, None),
        P("row", "col", None, None, None),
        P("row", "col", None, None),
        P("row", "col", None, None),
        P("row", "col", None, None),
        P("row", "col"),
    )
    out_specs = (P("row", "col", None, None, None), P("row", "col", None, None, None))
    return jax.shard_map(
        functools.partial(on_device, mesh.shape["row"], mesh.shape["col"]),
        mesh=mesh,
        in_specs=in_specs,
        out_specs=out_specs,
        check_vma=False,
    )
```
